256 devices in a mesh: span: 32 (over x_hi, z, core), seq: 8 (over y, x_lo).
Axes of the slice: x: 4 (x_hi: 2, x_lo: 2; x = x_hi * 2 + x_lo), y: 4, z: 8, core: 2. Of those that a mesh axis runs over, the one named last changes fastest.
Arguments:
- tokens: bfloat16 [65536, 1024], P(('span', 'seq')), may hold values from -48 to 48
- w_qkv: bfloat16 [1024, 3072], P('span'), may hold values from -0.1875 to 0.1875
- w_out: bfloat16 [1024, 1024], replicated, may hold values from -0.1875 to 0.1875
- w_cross: bfloat16 [1024, 2048], replicated, may hold values from -0.1875 to 0.1875
- ln_gain: float32 [1024], replicated, may hold values from 0.5 to 1.5
- ln_bias: float32 [1024], replicated, may hold values from -3 to 3
- queries: bfloat16 [1024, 1024], replicated, may hold values from -144 to 144
Outputs:
- encoded: bfloat16 [65536, 1024], P(('span', 'seq'))
- cross_out: bfloat16 [1024, 1024], P('span')
The draws below stay inside these ranges and needn't reach their ends.
All inputs are finite; a program needn't handle non-finite values.
Results may differ from the reference program's by a relative error of at most 0.013.
The reference program's roundings to bfloat16 on the way count: a program that leaves them out, or rounds other values in their place, can miss the bound.
Values may be sent and summed in bfloat16 or wider, within the bound.
No kernel may reach another device: no remote copies, remote signals or barrier semaphores. Data moves between devices by JAX's collectives and lax.ppermute only.
A program may use at most 128 MiB of HBM per device.

```python
import math
import jax
import jax.numpy as jnp
from jax import lax

D = 1024
H = 16
DH = 64
NQ = 1024
L = 2048
SPANS = 32
TOKENS = 65536


def draw_tokens(key, part):
    values = jnp.clip(jax.random.normal(jax.random.fold_in(key, 11), (TOKENS, D), jnp.float32), -6.0, 6.0)
    return values.astype(jnp.bfloat16)


def draw_queries(key, part):
    query_scale = 43.6 / math.sqrt(DH)
    values = query_scale * jnp.clip(jax.random.normal(jax.random.fold_in(key, 23), (NQ, D), jnp.float32), -4.0, 4.0)
    return values.astype(jnp.bfloat16)


def block_scale(own_key, extent, shards, low, high):
    def one(position, parts):
        heights = jax.random.uniform(jax.random.fold_in(jax.random.fold_in(own_key, 6), position), (parts,), jnp.float32, low / len(shards), high / len(shards))
        return jnp.repeat(jnp.exp(heights), extent[position] // parts).reshape((-1,) + (1,) * (len(extent) - position - 1))

    factor_of = one(*shards[0])
    for cut in shards[1:]:
        factor_of = factor_of * one(*cut)
    return factor_of


def gaussian(own_key, extent, deviation, bound, pieces=(), dtype=jnp.bfloat16):
    result = jax.random.normal(own_key, extent, jnp.float32) * deviation
    if len(pieces) > 0:
        result = block_scale(own_key, extent, pieces, -0.22, 0.18) * result
    return jnp.clip(result, min=-bound, max=bound).astype(dtype)


def setup_inputs(seed: int = 0) -> dict:
    streams_of = jax.random.split(jax.random.key(seed), 8)
    tokens = draw_tokens(jax.random.fold_in(streams_of[7], 71), 0)
    w_qkv = gaussian(streams_of[1], (D, 3 * D), D ** -0.5, 0.1875, ((0, 32),))
    w_out = gaussian(streams_of[2], (D, D), D ** -0.5, 0.1875)
    w_cross = gaussian(streams_of[3], (D, 2 * D), D ** -0.5, 0.1875)
    ln_gain = jnp.clip(jax.random.uniform(streams_of[4], (D,), jnp.float32, 0.5, 1.5), 0.5, 1.5)
    ln_bias = gaussian(streams_of[5], (D,), 0.5, 3.0, (), jnp.float32)
    queries = draw_queries(jax.random.fold_in(streams_of[7], 71), 0)
    return dict(tokens=tokens, w_qkv=w_qkv, w_out=w_out, w_cross=w_cross, ln_gain=ln_gain, ln_bias=ln_bias, queries=queries)


score_scale = 0.125

def layer_norm(residual, ln_gain, ln_bias):
    center = residual - lax.optimization_barrier(jnp.mean(residual, -1, keepdims=True))
    spread = lax.optimization_barrier(jnp.mean(center * center, -1, keepdims=True))
    return center * lax.rsqrt(spread + 1e-05) * ln_gain + ln_bias

def head_attend(triple):
    scores = jnp.dot(triple[0], triple[1].T, preferred_element_type=jnp.float32) * score_scale
    peaks = lax.optimization_barrier(jnp.max(scores, -1, keepdims=True))
    powers = jnp.exp(scores - peaks)
    totals = lax.optimization_barrier(jnp.sum(powers, -1, keepdims=True))
    return (jnp.dot(powers.astype(jnp.bfloat16), triple[2], preferred_element_type=jnp.float32) / totals).astype(jnp.bfloat16)

def reference(tokens, w_qkv, w_out, w_cross, ln_gain, ln_bias, queries):

    def encode_span(span_tokens):
        projected = jnp.dot(span_tokens, w_qkv, preferred_element_type=jnp.float32).astype(jnp.bfloat16)
        per_head = jnp.transpose(projected.reshape(L, 3, H, DH), (2, 1, 0, 3))
        head_outputs = lax.map(lambda triple: head_attend((triple[0], triple[1], triple[2])), per_head)
        attn = jnp.transpose(head_outputs, (1, 0, 2)).reshape(L, D)
        residual = span_tokens.astype(jnp.float32) + jnp.dot(attn, w_out, preferred_element_type=jnp.float32)
        encoded = layer_norm(residual, ln_gain, ln_bias).astype(jnp.bfloat16)
        cross_kv = jnp.dot(encoded, w_cross, preferred_element_type=jnp.float32).astype(jnp.bfloat16)
        return (encoded, cross_kv)
    encoded, cross_kv = lax.map(encode_span, tokens.reshape(SPANS, L, D))
    cross_kv = cross_kv.reshape(TOKENS, 2 * D)
    key_heads = jnp.transpose(cross_kv[:, :D].reshape(TOKENS, H, DH), (1, 0, 2))
    value_heads = jnp.transpose(cross_kv[:, D:].reshape(TOKENS, H, DH), (1, 0, 2))
    query_heads = jnp.transpose(queries.reshape(NQ, H, DH), (1, 0, 2))
    cross_heads = lax.map(lambda triple: head_attend((triple[0], triple[1], triple[2])), (query_heads, key_heads, value_heads))
    cross_out = jnp.transpose(cross_heads, (1, 0, 2)).reshape(NQ, D)
    return (encoded.reshape(TOKENS, D), cross_out)
```

```python
import functools
import math

import jax
import jax.numpy as jnp
from jax import lax
from jax.experimental import pallas as pl
from jax.experimental.pallas import tpu as pltpu
from jax.sharding import PartitionSpec as P

H = 16
DH = 64
PAIR = 2 * DH
MODEL = 1024
ROWS = 256
SEQ = 8
SPAN = 32
OWN = 32
NQ = 1024
STAT_LANES = 16
score_scale = 0.125
LOG2E = math.log2(math.e)
EXP2_SCALE = score_scale * LOG2E

bf16 = jnp.bfloat16
f32 = jnp.float32


def dot(a, b):
    return jnp.dot(a, b, preferred_element_type=f32)


def params(mib=48):
    return pltpu.CompilerParams(vmem_limit_bytes=mib * 1024 * 1024)


def permute(x, axis, size, target):
    return lax.ppermute(x, axis, [(i, target(i)) for i in range(size)])


def lane_low(shape):
    return lax.broadcasted_iota(jnp.int32, shape, len(shape) - 1) < DH


def gather_weight(w, seq_index, span_index):
    mine = lax.dynamic_slice_in_dim(w.reshape(32, 3, MODEL), seq_index * PAIR, PAIR, 2)
    mine = mine.reshape(1, 32, 3 * PAIR)
    x_hi = span_index // 16
    core = span_index % 2
    other = permute(mine, "span", SPAN, lambda i: i ^ 16)
    both = jnp.where(x_hi == 0, jnp.concatenate([mine, other]), jnp.concatenate([other, mine]))
    z_groups = {}
    for i in range(SPAN):
        z_groups.setdefault((i // 16, i % 2), []).append(i)
    ring = lax.all_to_all(
        jnp.broadcast_to(both[None], (8,) + both.shape),
        "span",
        split_axis=0,
        concat_axis=0,
        tiled=True,
        axis_index_groups=list(z_groups.values()),
    )
    twin = permute(ring, "span", SPAN, lambda i: i ^ 1)
    even = jnp.where(core == 0, ring, twin)
    odd = jnp.where(core == 0, twin, ring)
    whole = jnp.stack([even, odd], axis=2)
    return jnp.transpose(whole, (1, 0, 2, 3, 4)).reshape(MODEL, 3 * PAIR)


def gather_column(x):
    half = x.shape[0] // 2
    up = permute(x, "seq", SEQ, lambda i: (i + 2) % SEQ)
    down = permute(x, "seq", SEQ, lambda i: (i - 2) % SEQ)
    up_far = permute(up[:half], "seq", SEQ, lambda i: (i + 2) % SEQ)
    down_far = permute(down[half:], "seq", SEQ, lambda i: (i - 2) % SEQ)
    return up, down, up_far, down_far


def project_kernel(own, peer, up, down, up_far, down_far, w, out):
    row = 0
    for piece in (own, peer, up, down, up_far, down_far):
        count = piece.shape[0]
        out[row : row + count, :] = dot(piece[...], w[...]).astype(bf16)
        row += count


def softmax_pair(q, k_t, v_ones):
    low = lane_low(q.shape)
    zero = jnp.zeros_like(q)
    mixed, total, peak = [], [], []
    for h in range(2):
        scores = dot(jnp.where(low, q, zero) if h == 0 else jnp.where(low, zero, q), k_t)
        top = jnp.max(scores, axis=-1, keepdims=True)
        probs = jnp.exp2((scores - top) * EXP2_SCALE).astype(bf16)
        both = dot(probs, v_ones)
        mixed.append(both[:, :PAIR])
        total.append(both[:, PAIR:])
        peak.append(top)
    return (
        jnp.where(low, mixed[0], mixed[1]),
        jnp.where(low, total[0], total[1]),
        jnp.where(low, peak[0], peak[1]),
    )


def attend_kernel(table, early, up, down, up_far, down_far, w, out, q_all, k_t, v_ones):
    del table
    step = pl.program_id(0)

    @pl.when(step == 0)
    def _():
        v_ones[:, PAIR:] = jnp.ones_like(v_ones[:, PAIR:])
        done = early.shape[0]
        q_all[:done, :] = early[:, :PAIR]
        k_t[:, :done] = early[:, PAIR : 2 * PAIR].T
        v_ones[:done, :PAIR] = early[:, 2 * PAIR :]
        row = done
        for piece in (up, down, up_far, down_far):
            count = piece.shape[0]
            block = dot(piece[...], w[...]).astype(bf16)
            q_all[row : row + count, :] = block[:, :PAIR]
            k_t[:, row : row + count] = block[:, PAIR : 2 * PAIR].T
            v_ones[row : row + count, :PAIR] = block[:, 2 * PAIR :]
            row += count

    q = q_all[pl.ds(pl.multiple_of(step * ROWS, ROWS), ROWS), :]
    mixed, total, _ = softmax_pair(q, k_t[...], v_ones[...])
    out[0] = (mixed / total).astype(bf16)


def encode_kernel(attn, tokens, w_out, gain, bias, w_key, w_value, encoded, cross_kv):
    @pl.when(pl.program_id(0) == 0)
    def _():
        joined = jnp.concatenate([attn[p] for p in range(SEQ)], axis=1)
        residual = tokens[...].astype(f32) + dot(joined, w_out[...])
        center = residual - jnp.mean(residual, -1, keepdims=True)
        spread = jnp.mean(center * center, -1, keepdims=True)
        encoded[...] = (center * lax.rsqrt(spread + 1e-05) * gain[...] + bias[...]).astype(bf16)

    keys = dot(encoded[...], w_key[...]).astype(bf16)
    values = dot(encoded[...], w_value[...]).astype(bf16)
    for p in range(2):
        cross_kv[p, :, :PAIR] = keys[:, p * PAIR : (p + 1) * PAIR]
        cross_kv[p, :, PAIR:] = values[:, p * PAIR : (p + 1) * PAIR]


def cross_kernel(place, queries, kv, keep, send, k_t, v_ones):
    @pl.when(pl.program_id(0) == 0)
    def _():
        k_t[...] = kv[:, :PAIR].T
        v_ones[:, :PAIR] = kv[:, PAIR:]
        v_ones[:, PAIR:] = jnp.ones_like(v_ones[:, PAIR:])

    mixed, total, peak = softmax_pair(queries[...], k_t[...], v_ones[...])
    mixed = mixed / total
    weight = peak * score_scale + jnp.log(total)
    is_even = place[1] == 0
    for g in range(queries.shape[0] // (2 * OWN)):
        even = slice(2 * g * OWN, (2 * g + 1) * OWN)
        odd = slice((2 * g + 1) * OWN, (2 * g + 2) * OWN)
        rows = slice(g * OWN, (g + 1) * OWN)
        for lanes, value in ((slice(0, PAIR), mixed), (slice(PAIR, 2 * PAIR), weight)):
            keep[rows, lanes] = jnp.where(is_even, value[even], value[odd])
            send[rows, lanes] = jnp.where(is_even, value[odd], value[even])


def merge_kernel(keep, received, out):
    here, there = keep[:, PAIR:], received[:, PAIR:]
    top = jnp.maximum(here, there)
    scale_here, scale_there = jnp.exp(here - top), jnp.exp(there - top)
    total = scale_here + scale_there
    mixed = (keep[:, :PAIR] * scale_here + received[:, :PAIR] * scale_there) / total
    weight = top + jnp.log(total)
    high = weight.astype(bf16)
    rest = weight - high.astype(f32)
    middle = rest.astype(bf16)
    low = (rest - middle.astype(f32)).astype(bf16)
    part = lax.broadcasted_iota(jnp.int32, weight.shape, 1) % DH // STAT_LANES
    out[:, :PAIR] = mixed.astype(bf16)
    out[:, PAIR:] = jnp.where(part == 0, high, jnp.where(part == 1, middle, low))


def finish_kernel(parts, out):
    stat = parts[:, :, PAIR:].astype(f32)
    low = lane_low(stat.shape)
    columns = []
    for h in range(2):
        high, middle, rest = (
            stat[:, :, h * DH + p * STAT_LANES : h * DH + p * STAT_LANES + 1] for p in range(3)
        )
        columns.append(high + (middle + rest))
    weight = jnp.where(low, columns[0], columns[1])
    scale = jnp.exp(weight - jnp.max(weight, axis=0, keepdims=True))
    mixed = jnp.sum(parts[:, :, :PAIR].astype(f32) * scale, axis=0) / jnp.sum(scale, axis=0)
    out[...] = jnp.broadcast_to(mixed.astype(bf16)[None], out.shape)


def per_device(tokens, w_qkv, w_out, w_cross, ln_gain, ln_bias, queries):
    seq_index = lax.axis_index("seq")
    span_index = lax.axis_index("span")
    y, x_lo = seq_index // 2, seq_index % 2

    peer = permute(tokens, "seq", SEQ, lambda i: i ^ 1)
    near = gather_column(tokens)
    far = gather_column(peer)
    weight = gather_weight(w_qkv, seq_index, span_index)

    def whole(shape):
        return pl.BlockSpec(shape, lambda *_: (0,) * len(shape))

    early_rows = 5 * ROWS
    early = pl.pallas_call(
        project_kernel,
        out_shape=jax.ShapeDtypeStruct((early_rows, 3 * PAIR), bf16),
        compiler_params=params(),
        cost_estimate=pl.CostEstimate(
            flops=2 * early_rows * MODEL * 3 * PAIR, bytes_accessed=4 << 20, transcendentals=0
        ),
    )(tokens, peer, *near, weight)

    order = jnp.stack(
        [((y + dy) % 4) * 2 + (x_lo ^ flip) for dy, flip in
         ((0, 0), (0, 1), (3, 0), (1, 0), (2, 0), (3, 1), (1, 1), (2, 1))]
    ).astype(jnp.int32)
    length = SEQ * ROWS
    attn = pl.pallas_call(
        attend_kernel,
        grid_spec=pltpu.PrefetchScalarGridSpec(
            num_scalar_prefetch=1,
            grid=(SEQ,),
            in_specs=[
                whole((early_rows, 3 * PAIR)),
                whole((ROWS, MODEL)),
                whole((ROWS, MODEL)),
                whole((ROWS // 2, MODEL)),
                whole((ROWS // 2, MODEL)),
                whole((MODEL, 3 * PAIR)),
            ],
            out_specs=pl.BlockSpec((1, ROWS, PAIR), lambda b, table: (table[b], 0, 0)),
            scratch_shapes=[
                pltpu.VMEM((length, PAIR), bf16),
                pltpu.VMEM((PAIR, length), bf16),
                pltpu.VMEM((length, 2 * PAIR), bf16),
            ],
        ),
        out_shape=jax.ShapeDtypeStruct((SEQ, ROWS, PAIR), bf16),
        compiler_params=params(),
        cost_estimate=pl.CostEstimate(
            flops=8 * length * length * 2 * PAIR, bytes_accessed=4 << 20,
            transcendentals=2 * length * length,
        ),
    )(order, early, *far, weight)
    attn = lax.all_to_all(attn, "seq", split_axis=0, concat_axis=0, tiled=True)

    encoded, cross_kv = pl.pallas_call(
        encode_kernel,
        grid=(4,),
        in_specs=[
            whole((SEQ, ROWS, PAIR)),
            whole((ROWS, MODEL)),
            whole((MODEL, MODEL)),
            whole((1, MODEL)),
            whole((1, MODEL)),
            pl.BlockSpec((MODEL, 2 * PAIR), lambda g: (0, g)),
            pl.BlockSpec((MODEL, 2 * PAIR), lambda g: (0, 4 + g)),
        ],
        out_specs=[
            whole((ROWS, MODEL)),
            pl.BlockSpec((2, ROWS, 2 * PAIR), lambda g: (g, 0, 0)),
        ],
        out_shape=[
            jax.ShapeDtypeStruct((ROWS, MODEL), bf16),
            jax.ShapeDtypeStruct((SEQ, ROWS, 2 * PAIR), bf16),
        ],
        compiler_params=params(),
        cost_estimate=pl.CostEstimate(
            flops=2 * ROWS * MODEL * 3 * MODEL, bytes_accessed=8 << 20, transcendentals=0
        ),
    )(attn, tokens, w_out, ln_gain[None], ln_bias[None], w_cross, w_cross)

    kv = lax.all_to_all(cross_kv, "seq", split_axis=0, concat_axis=0, tiled=True)
    kv = kv.reshape(length, 2 * PAIR)

    place = jnp.stack([seq_index, span_index % 2]).astype(jnp.int32)
    blocks = NQ // ROWS
    keep, send = pl.pallas_call(
        cross_kernel,
        grid_spec=pltpu.PrefetchScalarGridSpec(
            num_scalar_prefetch=1,
            grid=(blocks,),
            in_specs=[
                pl.BlockSpec((ROWS, PAIR), lambda b, place: (b, place[0])),
                whole((length, 2 * PAIR)),
            ],
            out_specs=[
                pl.BlockSpec((ROWS // 2, 2 * PAIR), lambda b, place: (b, 0)),
                pl.BlockSpec((ROWS // 2, 2 * PAIR), lambda b, place: (b, 0)),
            ],
            scratch_shapes=[
                pltpu.VMEM((PAIR, length), bf16),
                pltpu.VMEM((length, 2 * PAIR), bf16),
            ],
        ),
        out_shape=[jax.ShapeDtypeStruct((NQ // 2, 2 * PAIR), f32)] * 2,
        compiler_params=params(),
        cost_estimate=pl.CostEstimate(
            flops=8 * NQ * length * 2 * PAIR, bytes_accessed=2 << 20,
            transcendentals=2 * NQ * length,
        ),
    )(place, queries, kv)

    received = permute(send, "span", SPAN, lambda i: i ^ 1)
    merged = pl.pallas_call(
        merge_kernel,
        out_shape=jax.ShapeDtypeStruct((NQ // 2, 2 * PAIR), bf16),
        compiler_params=params(),
    )(keep, received)
    parts = lax.all_to_all(
        merged.reshape(16, OWN, 2 * PAIR),
        "span",
        split_axis=0,
        concat_axis=0,
        tiled=True,
        axis_index_groups=[list(range(0, SPAN, 2)), list(range(1, SPAN, 2))],
    )
    mine = pl.pallas_call(
        finish_kernel,
        out_shape=jax.ShapeDtypeStruct((SEQ, OWN, PAIR), bf16),
        compiler_params=params(),
    )(parts)
    heads = lax.all_to_all(mine, "seq", split_axis=0, concat_axis=0, tiled=True)
    cross_out = jnp.transpose(heads, (1, 0, 2)).reshape(OWN, MODEL)
    return encoded, cross_out


def solution(mesh):
    in_specs = (P(("span", "seq"), None), P("span", None), P(), P(), P(), P(), P())
    out_specs = (P(("span", "seq"), None), P("span", None))
    return jax.shard_map(
        per_device, mesh=mesh, in_specs=in_specs, out_specs=out_specs, check_vma=False
    )
```

```python
import functools
import math

import jax
import jax.numpy as jnp
from jax import lax
from jax.experimental import pallas as pl
from jax.experimental.pallas import tpu as pltpu
from jax.sharding import PartitionSpec as P

H = 16
DH = 64
PAIR = 2 * DH
MODEL = 1024
ROWS = 256
SEQ = 8
SPAN = 32
OWN = 32
NQ = 1024
STAT_LANES = 16
BLOCK = 512
SPREAD = (16, 8, 4, 2)
score_scale = 0.125
LOG2E = math.log2(math.e)
EXP2_SCALE = score_scale * LOG2E

bf16 = jnp.bfloat16
f32 = jnp.float32


def dot(a, b):
    return jnp.dot(a, b, preferred_element_type=f32)


def params(mib=48):
    return pltpu.CompilerParams(vmem_limit_bytes=mib * 1024 * 1024)


def permute(x, axis, size, target):
    return lax.ppermute(x, axis, [(i, target(i)) for i in range(size)])


def lane_low(shape):
    return lax.broadcasted_iota(jnp.int32, shape, len(shape) - 1) < DH


def spread(blocks, bit):
    return jnp.concatenate([blocks, permute(blocks, "span", SPAN, lambda i: i ^ bit)])


def from_below(x):
    return permute(x, "seq", SEQ, lambda i: (i + 2) % SEQ)


def from_above(x):
    return permute(x, "seq", SEQ, lambda i: (i - 2) % SEQ)


def across(x):
    return permute(x, "seq", SEQ, lambda i: i ^ 1)


def project_kernel(place, own, peer, up, down, up_far, down_far, mine, twin, out, w):
    for k in range(1 << len(SPREAD)):
        flip = sum(bit for p, bit in enumerate(SPREAD) if k >> p & 1)
        for core, blocks in enumerate((mine, twin)):
            start = pl.multiple_of((place[1] ^ (flip + core)) * 32, 32)
            w[pl.ds(start, 32), :] = blocks[k * 32 : (k + 1) * 32, :]
    row = 0
    for piece in (own, peer, up, down, up_far, down_far):
        count = piece.shape[0]
        out[row : row + count, :] = dot(piece[...], w[...]).astype(bf16)
        row += count


def head_scores(q, k_t, head):
    low = lane_low(q.shape)
    zero = jnp.zeros_like(q)
    return dot(jnp.where(low, q, zero) if head == 0 else jnp.where(low, zero, q), k_t)


def weigh(scores, v_ones):
    top = jnp.max(scores, axis=-1, keepdims=True)
    probs = jnp.exp2((scores - top) * EXP2_SCALE).astype(bf16)
    return dot(probs, v_ones), top


def softmax_pair(step, q_block, k_t, v_ones, scores_0, scores_1):
    scores_1[...] = head_scores(q_block(step), k_t[...], 1)
    mixed_0, peak_0 = weigh(scores_0[...], v_ones[...])
    after = jnp.minimum(step + 1, pl.num_programs(0) - 1)
    scores_0[...] = head_scores(q_block(after), k_t[...], 0)
    mixed_1, peak_1 = weigh(scores_1[...], v_ones[...])
    low = lane_low((scores_0.shape[0], PAIR))
    total = jnp.where(low, mixed_0[:, PAIR:], mixed_1[:, PAIR:])
    mixed = jnp.where(low, mixed_0[:, :PAIR], mixed_1[:, :PAIR]) / total
    return mixed, total, jnp.where(low, peak_0, peak_1)


def attend_kernel(
    table, early, up, down, up_far, down_far, w, out, q_all, k_t, v_ones, scores_0, scores_1
):
    step = pl.program_id(0)

    def q_block(i):
        return q_all[pl.ds(pl.multiple_of(i * BLOCK, BLOCK), BLOCK), :]

    @pl.when(step == 0)
    def _():
        v_ones[:, PAIR:] = jnp.ones_like(v_ones[:, PAIR:])
        done = early.shape[0]
        q_all[:done, :] = early[:, :PAIR]
        k_t[:, :done] = early[:, PAIR : 2 * PAIR].T
        v_ones[:done, :PAIR] = early[:, 2 * PAIR :]
        row = done
        for piece in (up, down, up_far, down_far):
            count = piece.shape[0]
            block = dot(piece[...], w[...]).astype(bf16)
            q_all[row : row + count, :] = block[:, :PAIR]
            k_t[:, row : row + count] = block[:, PAIR : 2 * PAIR].T
            v_ones[row : row + count, :PAIR] = block[:, 2 * PAIR :]
            row += count
        scores_0[...] = head_scores(q_block(0), k_t[...], 0)

    mixed, _, _ = softmax_pair(step, q_block, k_t, v_ones, scores_0, scores_1)
    mixed = mixed.astype(bf16)
    for p in range(BLOCK // ROWS):
        out[table[step * (BLOCK // ROWS) + p]] = mixed[p * ROWS : (p + 1) * ROWS]


def encode_kernel(attn, tokens, w_out, gain, bias, w_cross, encoded, cross_kv):
    joined = jnp.concatenate([attn[p] for p in range(SEQ)], axis=1)
    residual = tokens[...].astype(f32) + dot(joined, w_out[...])
    center = residual - jnp.mean(residual, -1, keepdims=True)
    spread = jnp.mean(center * center, -1, keepdims=True)
    state = (center * lax.rsqrt(spread + 1e-05) * gain[...] + bias[...]).astype(bf16)
    encoded[...] = state
    for g in range(SEQ // 2):
        for part in range(2):
            start = part * MODEL + 2 * g * PAIR
            both = dot(state, w_cross[:, start : start + 2 * PAIR]).astype(bf16)
            for p in range(2):
                cross_kv[2 * g + p, :, part * PAIR : (part + 1) * PAIR] = both[
                    :, p * PAIR : (p + 1) * PAIR
                ]


def cross_kernel(place, queries, kv, keep, send, k_t, v_ones, scores_0, scores_1):
    step = pl.program_id(0)

    def q_block(i):
        return queries[pl.ds(pl.multiple_of(i * BLOCK, BLOCK), BLOCK), :]

    @pl.when(step == 0)
    def _():
        k_t[...] = kv[:, :PAIR].T
        v_ones[:, :PAIR] = kv[:, PAIR:]
        v_ones[:, PAIR:] = jnp.ones_like(v_ones[:, PAIR:])
        scores_0[...] = head_scores(q_block(0), k_t[...], 0)

    mixed, total, peak = softmax_pair(step, q_block, k_t, v_ones, scores_0, scores_1)
    weight = peak * score_scale + jnp.log(total)
    is_even = place[1] % 2 == 0
    for g in range(BLOCK // (2 * OWN)):
        even = slice(2 * g * OWN, (2 * g + 1) * OWN)
        odd = slice((2 * g + 1) * OWN, (2 * g + 2) * OWN)
        rows = slice(g * OWN, (g + 1) * OWN)
        for lanes, value in ((slice(0, PAIR), mixed), (slice(PAIR, 2 * PAIR), weight)):
            keep[rows, lanes] = jnp.where(is_even, value[even], value[odd])
            send[rows, lanes] = jnp.where(is_even, value[odd], value[even])


def merge_kernel(keep, received, out):
    here, there = keep[:, PAIR:], received[:, PAIR:]
    top = jnp.maximum(here, there)
    scale_here, scale_there = jnp.exp(here - top), jnp.exp(there - top)
    total = scale_here + scale_there
    mixed = (keep[:, :PAIR] * scale_here + received[:, :PAIR] * scale_there) / total
    weight = top + jnp.log(total)
    high = weight.astype(bf16)
    rest = weight - high.astype(f32)
    middle = rest.astype(bf16)
    low = (rest - middle.astype(f32)).astype(bf16)
    part = lax.broadcasted_iota(jnp.int32, weight.shape, 1) % DH // STAT_LANES
    out[:, :PAIR] = mixed.astype(bf16)
    out[:, PAIR:] = jnp.where(part == 0, high, jnp.where(part == 1, middle, low))


def finish_kernel(parts, out):
    stat = parts[:, :, PAIR:].astype(f32)
    low = lane_low(stat.shape)
    columns = []
    for h in range(2):
        high, middle, rest = (
            stat[:, :, h * DH + p * STAT_LANES : h * DH + p * STAT_LANES + 1] for p in range(3)
        )
        columns.append(high + (middle + rest))
    weight = jnp.where(low, columns[0], columns[1])
    scale = jnp.exp(weight - jnp.max(weight, axis=0, keepdims=True))
    mixed = jnp.sum(parts[:, :, :PAIR].astype(f32) * scale, axis=0) / jnp.sum(scale, axis=0)
    out[...] = jnp.broadcast_to(mixed.astype(bf16)[None], out.shape)


def per_device(tokens, w_qkv, w_out, w_cross, ln_gain, ln_bias, queries):
    seq_index = lax.axis_index("seq")
    span_index = lax.axis_index("span")
    y, x_lo = seq_index // 2, seq_index % 2

    half = ROWS // 2
    peer, up, down = across(tokens), from_below(tokens), from_above(tokens)
    mine = lax.dynamic_slice_in_dim(w_qkv.reshape(32, 3, MODEL), seq_index * PAIR, PAIR, 2)
    mine = mine.reshape(32, 3 * PAIR)
    for bit in SPREAD[:2]:
        mine = spread(mine, bit)
    peer, up, down, mine = lax.optimization_barrier((peer, up, down, mine))
    far_up, far_down = from_below(peer), from_above(peer)
    near = (up, down, from_below(up[:half]), from_above(down[half:]))
    far = (far_up, far_down, across(near[2]), across(near[3]))
    for bit in SPREAD[2:]:
        mine = spread(mine, bit)
    twin = permute(mine, "span", SPAN, lambda i: i ^ 1)

    def whole(shape):
        return pl.BlockSpec(shape, lambda *_: (0,) * len(shape))

    place = jnp.stack([seq_index, span_index]).astype(jnp.int32)
    early_rows = 5 * ROWS
    early, weight = pl.pallas_call(
        project_kernel,
        in_specs=[pl.BlockSpec(memory_space=pltpu.SMEM)] + [pl.BlockSpec(memory_space=pltpu.VMEM)] * 8,
        out_shape=[
            jax.ShapeDtypeStruct((early_rows, 3 * PAIR), bf16),
            jax.ShapeDtypeStruct((MODEL, 3 * PAIR), bf16),
        ],
        compiler_params=params(),
        cost_estimate=pl.CostEstimate(
            flops=2 * early_rows * MODEL * 3 * PAIR, bytes_accessed=4 << 20, transcendentals=0
        ),
    )(place, tokens, peer, *near, mine, twin)

    order = jnp.stack(
        [((y + dy) % 4) * 2 + (x_lo ^ flip) for dy, flip in
         ((0, 0), (0, 1), (3, 0), (1, 0), (2, 0), (3, 1), (1, 1), (2, 1))]
    ).astype(jnp.int32)
    length = SEQ * ROWS
    attn = pl.pallas_call(
        attend_kernel,
        grid_spec=pltpu.PrefetchScalarGridSpec(
            num_scalar_prefetch=1,
            grid=(length // BLOCK,),
            in_specs=[
                whole((early_rows, 3 * PAIR)),
                whole((ROWS, MODEL)),
                whole((ROWS, MODEL)),
                whole((ROWS // 2, MODEL)),
                whole((ROWS // 2, MODEL)),
                whole((MODEL, 3 * PAIR)),
            ],
            out_specs=whole((SEQ, ROWS, PAIR)),
            scratch_shapes=[
                pltpu.VMEM((length, PAIR), bf16),
                pltpu.VMEM((PAIR, length), bf16),
                pltpu.VMEM((length, 2 * PAIR), bf16),
                pltpu.VMEM((BLOCK, length), f32),
                pltpu.VMEM((BLOCK, length), f32),
            ],
        ),
        out_shape=jax.ShapeDtypeStruct((SEQ, ROWS, PAIR), bf16),
        compiler_params=params(),
        cost_estimate=pl.CostEstimate(
            flops=8 * length * length * 2 * PAIR, bytes_accessed=4 << 20,
            transcendentals=2 * length * length,
        ),
    )(order, early, *far, weight)
    attn = lax.all_to_all(attn, "seq", split_axis=0, concat_axis=0, tiled=True)

    encoded, cross_kv = pl.pallas_call(
        encode_kernel,
        out_shape=[
            jax.ShapeDtypeStruct((ROWS, MODEL), bf16),
            jax.ShapeDtypeStruct((SEQ, ROWS, 2 * PAIR), bf16),
        ],
        compiler_params=params(),
        cost_estimate=pl.CostEstimate(
            flops=2 * ROWS * MODEL * 3 * MODEL, bytes_accessed=8 << 20, transcendentals=0
        ),
    )(attn, tokens, w_out, ln_gain[None], ln_bias[None], w_cross)

    kv = lax.all_to_all(cross_kv, "seq", split_axis=0, concat_axis=0, tiled=True)
    kv = kv.reshape(length, 2 * PAIR)

    blocks = NQ // BLOCK
    keep, send = pl.pallas_call(
        cross_kernel,
        grid_spec=pltpu.PrefetchScalarGridSpec(
            num_scalar_prefetch=1,
            grid=(blocks,),
            in_specs=[
                pl.BlockSpec((NQ, PAIR), lambda b, place: (0, place[0])),
                whole((length, 2 * PAIR)),
            ],
            out_specs=[
                pl.BlockSpec((BLOCK // 2, 2 * PAIR), lambda b, place: (b, 0)),
                pl.BlockSpec((BLOCK // 2, 2 * PAIR), lambda b, place: (b, 0)),
            ],
            scratch_shapes=[
                pltpu.VMEM((PAIR, length), bf16),
                pltpu.VMEM((length, 2 * PAIR), bf16),
                pltpu.VMEM((BLOCK, length), f32),
                pltpu.VMEM((BLOCK, length), f32),
            ],
        ),
        out_shape=[jax.ShapeDtypeStruct((NQ // 2, 2 * PAIR), f32)] * 2,
        compiler_params=params(),
        cost_estimate=pl.CostEstimate(
            flops=8 * NQ * length * 2 * PAIR, bytes_accessed=2 << 20,
            transcendentals=2 * NQ * length,
        ),
    )(place, queries, kv)

    received = permute(send, "span", SPAN, lambda i: i ^ 1)
    merged = pl.pallas_call(
        merge_kernel,
        out_shape=jax.ShapeDtypeStruct((NQ // 2, 2 * PAIR), bf16),
        compiler_params=params(),
    )(keep, received)
    parts = lax.all_to_all(
        merged.reshape(16, OWN, 2 * PAIR),
        "span",
        split_axis=0,
        concat_axis=0,
        tiled=True,
        axis_index_groups=[list(range(0, SPAN, 2)), list(range(1, SPAN, 2))],
    )
    mine = pl.pallas_call(
        finish_kernel,
        out_shape=jax.ShapeDtypeStruct((SEQ, OWN, PAIR), bf16),
        compiler_params=params(),
    )(parts)
    heads = lax.all_to_all(mine, "seq", split_axis=0, concat_axis=0, tiled=True)
    cross_out = jnp.transpose(heads, (1, 0, 2)).reshape(OWN, MODEL)
    return encoded, cross_out


def solution(mesh):
    in_specs = (P(("span", "seq"), None), P("span", None), P(), P(), P(), P(), P())
    out_specs = (P(("span", "seq"), None), P("span", None))
    return jax.shard_map(
        per_device, mesh=mesh, in_specs=in_specs, out_specs=out_specs, check_vma=False
    )
```

```python
import functools
import math

import jax
import jax.numpy as jnp
from jax import lax
from jax.experimental import pallas as pl
from jax.experimental.pallas import tpu as pltpu
from jax.sharding import PartitionSpec as P

H = 16
DH = 64
PAIR = 2 * DH
MODEL = 1024
ROWS = 256
SEQ = 8
SPAN = 32
OWN = 32
NQ = 1024
STAT_LANES = 16
BLOCK = 512
SPREAD = (8, 4, 2, 16)
score_scale = 0.125
LOG2E = math.log2(math.e)
EXP2_SCALE = score_scale * LOG2E

bf16 = jnp.bfloat16
f32 = jnp.float32


def dot(a, b):
    return jnp.dot(a, b, preferred_element_type=f32)


def params(mib=48):
    return pltpu.CompilerParams(vmem_limit_bytes=mib * 1024 * 1024)


def permute(x, axis, size, target):
    return lax.ppermute(x, axis, [(i, target(i)) for i in range(size)])


def lane_low(shape):
    return lax.broadcasted_iota(jnp.int32, shape, len(shape) - 1) < DH


def spread(blocks, bits):
    flips = (bits[0], bits[1], bits[0] | bits[1])
    return jnp.concatenate([blocks] + [permute(blocks, "span", SPAN, lambda i, f=f: i ^ f) for f in flips])


def from_below(x):
    return permute(x, "seq", SEQ, lambda i: (i + 2) % SEQ)


def from_above(x):
    return permute(x, "seq", SEQ, lambda i: (i - 2) % SEQ)


def across(x):
    return permute(x, "seq", SEQ, lambda i: i ^ 1)


def project_kernel(place, own, peer, up, down, up_far, down_far, mine, twin, out, w):
    for k in range(1 << len(SPREAD)):
        flip = sum(bit for p, bit in enumerate(SPREAD) if k >> p & 1)
        for core, blocks in enumerate((mine, twin)):
            start = pl.multiple_of((place[1] ^ (flip + core)) * 32, 32)
            w[pl.ds(start, 32), :] = blocks[k * 32 : (k + 1) * 32, :]
    row = 0
    for piece in (own, peer, up, down, up_far, down_far):
        count = piece.shape[0]
        out[row : row + count, :] = dot(piece[...], w[...]).astype(bf16)
        row += count


def head_scores(q, k_t, head):
    low = lane_low(q.shape)
    zero = jnp.zeros_like(q)
    return dot(jnp.where(low, q, zero) if head == 0 else jnp.where(low, zero, q), k_t)


def weigh(scores, v_ones):
    top = jnp.max(scores, axis=-1, keepdims=True)
    probs = jnp.exp2((scores - top) * EXP2_SCALE).astype(bf16)
    return dot(probs, v_ones), top


def softmax_pair(step, q_block, k_t, v_ones, scores_0, scores_1):
    scores_1[...] = head_scores(q_block(step), k_t[...], 1)
    mixed_0, peak_0 = weigh(scores_0[...], v_ones[...])
    after = jnp.minimum(step + 1, pl.num_programs(0) - 1)
    scores_0[...] = head_scores(q_block(after), k_t[...], 0)
    mixed_1, peak_1 = weigh(scores_1[...], v_ones[...])
    low = lane_low((scores_0.shape[0], PAIR))
    total = jnp.where(low, mixed_0[:, PAIR:], mixed_1[:, PAIR:])
    mixed = jnp.where(low, mixed_0[:, :PAIR], mixed_1[:, :PAIR]) / total
    return mixed, total, jnp.where(low, peak_0, peak_1)


def attend_kernel(
    table, early, up, down, up_far, down_far, w, out, q_all, k_t, v_ones, scores_0, scores_1
):
    step = pl.program_id(0)

    def q_block(i):
        return q_all[pl.ds(pl.multiple_of(i * BLOCK, BLOCK), BLOCK), :]

    @pl.when(step == 0)
    def _():
        v_ones[:, PAIR:] = jnp.ones_like(v_ones[:, PAIR:])
        done = early.shape[0]
        q_all[:done, :] = early[:, :PAIR]
        k_t[:, :done] = early[:, PAIR : 2 * PAIR].T
        v_ones[:done, :PAIR] = early[:, 2 * PAIR :]
        row = done
        for piece in (up, down, up_far, down_far):
            count = piece.shape[0]
            block = dot(piece[...], w[...]).astype(bf16)
            q_all[row : row + count, :] = block[:, :PAIR]
            k_t[:, row : row + count] = block[:, PAIR : 2 * PAIR].T
            v_ones[row : row + count, :PAIR] = block[:, 2 * PAIR :]
            row += count
        scores_0[...] = head_scores(q_block(0), k_t[...], 0)

    mixed, _, _ = softmax_pair(step, q_block, k_t, v_ones, scores_0, scores_1)
    mixed = mixed.astype(bf16)
    for p in range(BLOCK // ROWS):
        out[table[step * (BLOCK // ROWS) + p]] = mixed[p * ROWS : (p + 1) * ROWS]


def encode_kernel(attn, tokens, w_out, gain, bias, w_cross, encoded, cross_kv):
    joined = jnp.concatenate([attn[p] for p in range(SEQ)], axis=1)
    residual = tokens[...].astype(f32) + dot(joined, w_out[...])
    center = residual - jnp.mean(residual, -1, keepdims=True)
    spread = jnp.mean(center * center, -1, keepdims=True)
    state = (center * lax.rsqrt(spread + 1e-05) * gain[...] + bias[...]).astype(bf16)
    encoded[...] = state
    for g in range(SEQ // 2):
        for part in range(2):
            start = part * MODEL + 2 * g * PAIR
            both = dot(state, w_cross[:, start : start + 2 * PAIR]).astype(bf16)
            for p in range(2):
                cross_kv[2 * g + p, :, part * PAIR : (part + 1) * PAIR] = both[
                    :, p * PAIR : (p + 1) * PAIR
                ]


def cross_kernel(place, queries, kv, keep, send, k_t, v_ones, scores_0, scores_1):
    step = pl.program_id(0)

    def q_block(i):
        return queries[pl.ds(pl.multiple_of(i * BLOCK, BLOCK), BLOCK), :]

    @pl.when(step == 0)
    def _():
        k_t[...] = kv[:, :PAIR].T
        v_ones[:, :PAIR] = kv[:, PAIR:]
        v_ones[:, PAIR:] = jnp.ones_like(v_ones[:, PAIR:])
        scores_0[...] = head_scores(q_block(0), k_t[...], 0)

    mixed, total, peak = softmax_pair(step, q_block, k_t, v_ones, scores_0, scores_1)
    weight = peak * score_scale + jnp.log(total)
    is_even = place[1] % 2 == 0
    for g in range(BLOCK // (2 * OWN)):
        even = slice(2 * g * OWN, (2 * g + 1) * OWN)
        odd = slice((2 * g + 1) * OWN, (2 * g + 2) * OWN)
        rows = slice(g * OWN, (g + 1) * OWN)
        for lanes, value in ((slice(0, PAIR), mixed), (slice(PAIR, 2 * PAIR), weight)):
            keep[rows, lanes] = jnp.where(is_even, value[even], value[odd])
            send[rows, lanes] = jnp.where(is_even, value[odd], value[even])


def merge_kernel(keep, received, out):
    here, there = keep[:, PAIR:], received[:, PAIR:]
    top = jnp.maximum(here, there)
    scale_here, scale_there = jnp.exp(here - top), jnp.exp(there - top)
    total = scale_here + scale_there
    mixed = (keep[:, :PAIR] * scale_here + received[:, :PAIR] * scale_there) / total
    weight = top + jnp.log(total)
    high = weight.astype(bf16)
    rest = weight - high.astype(f32)
    middle = rest.astype(bf16)
    low = (rest - middle.astype(f32)).astype(bf16)
    part = lax.broadcasted_iota(jnp.int32, weight.shape, 1) % DH // STAT_LANES
    out[:, :PAIR] = mixed.astype(bf16)
    out[:, PAIR:] = jnp.where(part == 0, high, jnp.where(part == 1, middle, low))


def finish_kernel(parts, out):
    stat = parts[:, :, PAIR:].astype(f32)
    low = lane_low(stat.shape)
    columns = []
    for h in range(2):
        high, middle, rest = (
            stat[:, :, h * DH + p * STAT_LANES : h * DH + p * STAT_LANES + 1] for p in range(3)
        )
        columns.append(high + (middle + rest))
    weight = jnp.where(low, columns[0], columns[1])
    scale = jnp.exp(weight - jnp.max(weight, axis=0, keepdims=True))
    mixed = jnp.sum(parts[:, :, :PAIR].astype(f32) * scale, axis=0) / jnp.sum(scale, axis=0)
    out[...] = jnp.broadcast_to(mixed.astype(bf16)[None], out.shape)


def per_device(tokens, w_qkv, w_out, w_cross, ln_gain, ln_bias, queries):
    seq_index = lax.axis_index("seq")
    span_index = lax.axis_index("span")
    y, x_lo = seq_index // 2, seq_index % 2

    half = ROWS // 2
    peer, up, down = across(tokens), from_below(tokens), from_above(tokens)
    mine = jnp.concatenate(
        [
            lax.dynamic_slice_in_dim(w_qkv, part * MODEL + seq_index * PAIR, PAIR, 1)
            for part in range(3)
        ],
        axis=1,
    )
    mine = spread(mine, SPREAD[:2])
    peer, up, down, mine = lax.optimization_barrier((peer, up, down, mine))
    near = (up, down, from_below(up[:half]), from_above(down[half:]))
    mine = spread(mine, SPREAD[2:])
    peer, mine = lax.optimization_barrier((peer, mine))
    far = (from_below(peer), from_above(peer), across(near[2]), across(near[3]))
    twin = permute(mine, "span", SPAN, lambda i: i ^ 1)

    def whole(shape):
        return pl.BlockSpec(shape, lambda *_: (0,) * len(shape))

    place = jnp.stack([seq_index, span_index]).astype(jnp.int32)
    early_rows = 5 * ROWS
    early, weight = pl.pallas_call(
        project_kernel,
        in_specs=[pl.BlockSpec(memory_space=pltpu.SMEM)] + [pl.BlockSpec(memory_space=pltpu.VMEM)] * 8,
        out_shape=[
            jax.ShapeDtypeStruct((early_rows, 3 * PAIR), bf16),
            jax.ShapeDtypeStruct((MODEL, 3 * PAIR), bf16),
        ],
        compiler_params=params(),
        cost_estimate=pl.CostEstimate(
            flops=2 * early_rows * MODEL * 3 * PAIR, bytes_accessed=4 << 20, transcendentals=0
        ),
    )(place, tokens, peer, *near, mine, twin)

    order = jnp.stack(
        [((y + dy) % 4) * 2 + (x_lo ^ flip) for dy, flip in
         ((0, 0), (0, 1), (3, 0), (1, 0), (2, 0), (3, 1), (1, 1), (2, 1))]
    ).astype(jnp.int32)
    length = SEQ * ROWS
    attn = pl.pallas_call(
        attend_kernel,
        grid_spec=pltpu.PrefetchScalarGridSpec(
            num_scalar_prefetch=1,
            grid=(length // BLOCK,),
            in_specs=[
                whole((early_rows, 3 * PAIR)),
                whole((ROWS, MODEL)),
                whole((ROWS, MODEL)),
                whole((ROWS // 2, MODEL)),
                whole((ROWS // 2, MODEL)),
                whole((MODEL, 3 * PAIR)),
            ],
            out_specs=whole((SEQ, ROWS, PAIR)),
            scratch_shapes=[
                pltpu.VMEM((length, PAIR), bf16),
                pltpu.VMEM((PAIR, length), bf16),
                pltpu.VMEM((length, 2 * PAIR), bf16),
                pltpu.VMEM((BLOCK, length), f32),
                pltpu.VMEM((BLOCK, length), f32),
            ],
        ),
        out_shape=jax.ShapeDtypeStruct((SEQ, ROWS, PAIR), bf16),
        compiler_params=params(),
        cost_estimate=pl.CostEstimate(
            flops=8 * length * length * 2 * PAIR, bytes_accessed=4 << 20,
            transcendentals=2 * length * length,
        ),
    )(order, early, *far, weight)
    attn = lax.all_to_all(attn, "seq", split_axis=0, concat_axis=0, tiled=True)

    encoded, cross_kv = pl.pallas_call(
        encode_kernel,
        out_shape=[
            jax.ShapeDtypeStruct((ROWS, MODEL), bf16),
            jax.ShapeDtypeStruct((SEQ, ROWS, 2 * PAIR), bf16),
        ],
        compiler_params=params(),
        cost_estimate=pl.CostEstimate(
            flops=2 * ROWS * MODEL * 3 * MODEL, bytes_accessed=8 << 20, transcendentals=0
        ),
    )(attn, tokens, w_out, ln_gain[None], ln_bias[None], w_cross)

    kv = lax.all_to_all(cross_kv, "seq", split_axis=0, concat_axis=0, tiled=True)
    kv = kv.reshape(length, 2 * PAIR)

    blocks = NQ // BLOCK
    keep, send = pl.pallas_call(
        cross_kernel,
        grid_spec=pltpu.PrefetchScalarGridSpec(
            num_scalar_prefetch=1,
            grid=(blocks,),
            in_specs=[
                pl.BlockSpec((NQ, PAIR), lambda b, place: (0, place[0])),
                whole((length, 2 * PAIR)),
            ],
            out_specs=[
                pl.BlockSpec((BLOCK // 2, 2 * PAIR), lambda b, place: (b, 0)),
                pl.BlockSpec((BLOCK // 2, 2 * PAIR), lambda b, place: (b, 0)),
            ],
            scratch_shapes=[
                pltpu.VMEM((PAIR, length), bf16),
                pltpu.VMEM((length, 2 * PAIR), bf16),
                pltpu.VMEM((BLOCK, length), f32),
                pltpu.VMEM((BLOCK, length), f32),
            ],
        ),
        out_shape=[jax.ShapeDtypeStruct((NQ // 2, 2 * PAIR), f32)] * 2,
        compiler_params=params(),
        cost_estimate=pl.CostEstimate(
            flops=8 * NQ * length * 2 * PAIR, bytes_accessed=2 << 20,
            transcendentals=2 * NQ * length,
        ),
    )(place, queries, kv)

    received = permute(send, "span", SPAN, lambda i: i ^ 1)
    merged = pl.pallas_call(
        merge_kernel,
        out_shape=jax.ShapeDtypeStruct((NQ // 2, 2 * PAIR), bf16),
        compiler_params=params(),
    )(keep, received)
    parts = lax.all_to_all(
        merged.reshape(16, OWN, 2 * PAIR),
        "span",
        split_axis=0,
        concat_axis=0,
        tiled=True,
        axis_index_groups=[list(range(0, SPAN, 2)), list(range(1, SPAN, 2))],
    )
    mine = pl.pallas_call(
        finish_kernel,
        out_shape=jax.ShapeDtypeStruct((SEQ, OWN, PAIR), bf16),
        compiler_params=params(),
    )(parts)
    heads = lax.all_to_all(mine, "seq", split_axis=0, concat_axis=0, tiled=True)
    cross_out = jnp.transpose(heads, (1, 0, 2)).reshape(OWN, MODEL)
    return encoded, cross_out


def solution(mesh):
    in_specs = (P(("span", "seq"), None), P("span", None), P(), P(), P(), P(), P())
    out_specs = (P(("span", "seq"), None), P("span", None))
    return jax.shard_map(
        per_device, mesh=mesh, in_specs=in_specs, out_specs=out_specs, check_vma=False
    )
```

```python
import functools
import math

import jax
import jax.numpy as jnp
from jax import lax
from jax.experimental import pallas as pl
from jax.experimental.pallas import tpu as pltpu
from jax.sharding import PartitionSpec as P

H = 16
DH = 64
PAIR = 2 * DH
MODEL = 1024
ROWS = 256
SEQ = 8
SPAN = 32
OWN = 32
NQ = 1024
STAT_LANES = 16
BLOCK = 512
Z_OFFSETS = (0, -1, 1, -3, -4, -2, 3, 2)
score_scale = 0.125
LOG2E = math.log2(math.e)
EXP2_SCALE = score_scale * LOG2E

bf16 = jnp.bfloat16
f32 = jnp.float32


def dot(a, b):
    return jnp.dot(a, b, preferred_element_type=f32)


def params(mib=48):
    return pltpu.CompilerParams(vmem_limit_bytes=mib * 1024 * 1024)


def permute(x, axis, size, target):
    return lax.ppermute(x, axis, [(i, target(i)) for i in range(size)])


def lane_low(shape):
    return lax.broadcasted_iota(jnp.int32, shape, len(shape) - 1) < DH


def along_z(blocks, step):
    def target(i):
        return (i & 17) | (((i >> 1) - step) % 8) << 1

    return permute(blocks, "span", SPAN, target)


def from_below(x):
    return permute(x, "seq", SEQ, lambda i: (i + 2) % SEQ)


def from_above(x):
    return permute(x, "seq", SEQ, lambda i: (i - 2) % SEQ)


def across(x):
    return permute(x, "seq", SEQ, lambda i: i ^ 1)


def project_kernel(place, own, peer, up, down, up_far, down_far, mine, twin, out, w):
    x_hi, z, side = place[1] // 16, place[1] // 2 % 8, place[1] % 2
    for k in range(2 * len(Z_OFFSETS)):
        across_x, offset = k // len(Z_OFFSETS), Z_OFFSETS[k % len(Z_OFFSETS)]
        for flip, blocks in enumerate((mine, twin)):
            block = ((x_hi ^ across_x) * 8 + (z + offset + 8) % 8) * 2 + (side ^ flip)
            start = pl.multiple_of(block * 32, 32)
            w[pl.ds(start, 32), :] = blocks[k * 32 : (k + 1) * 32, :]
    row = 0
    for piece in (own, peer, up, down, up_far, down_far):
        count = piece.shape[0]
        out[row : row + count, :] = dot(piece[...], w[...]).astype(bf16)
        row += count


def head_scores(q, k_t, head):
    low = lane_low(q.shape)
    zero = jnp.zeros_like(q)
    return dot(jnp.where(low, q, zero) if head == 0 else jnp.where(low, zero, q), k_t)


def weigh(scores, v_ones):
    top = jnp.max(scores, axis=-1, keepdims=True)
    probs = jnp.exp2((scores - top) * EXP2_SCALE).astype(bf16)
    return dot(probs, v_ones), top


def softmax_pair(step, q_block, k_t, v_ones, scores_0, scores_1):
    scores_1[...] = head_scores(q_block(step), k_t[...], 1)
    mixed_0, peak_0 = weigh(scores_0[...], v_ones[...])
    after = jnp.minimum(step + 1, pl.num_programs(0) - 1)
    scores_0[...] = head_scores(q_block(after), k_t[...], 0)
    mixed_1, peak_1 = weigh(scores_1[...], v_ones[...])
    low = lane_low((scores_0.shape[0], PAIR))
    total = jnp.where(low, mixed_0[:, PAIR:], mixed_1[:, PAIR:])
    mixed = jnp.where(low, mixed_0[:, :PAIR], mixed_1[:, :PAIR]) / total
    return mixed, total, jnp.where(low, peak_0, peak_1)


def attend_kernel(
    table, early, up, down, up_far, down_far, w, out, q_all, k_t, v_ones, scores_0, scores_1
):
    step = pl.program_id(0)

    def q_block(i):
        return q_all[pl.ds(pl.multiple_of(i * BLOCK, BLOCK), BLOCK), :]

    @pl.when(step == 0)
    def _():
        v_ones[:, PAIR:] = jnp.ones_like(v_ones[:, PAIR:])
        done = early.shape[0]
        q_all[:done, :] = early[:, :PAIR]
        k_t[:, :done] = early[:, PAIR : 2 * PAIR].T
        v_ones[:done, :PAIR] = early[:, 2 * PAIR :]
        row = done
        for piece in (up, down, up_far, down_far):
            count = piece.shape[0]
            block = dot(piece[...], w[...]).astype(bf16)
            q_all[row : row + count, :] = block[:, :PAIR]
            k_t[:, row : row + count] = block[:, PAIR : 2 * PAIR].T
            v_ones[row : row + count, :PAIR] = block[:, 2 * PAIR :]
            row += count
        scores_0[...] = head_scores(q_block(0), k_t[...], 0)

    mixed, _, _ = softmax_pair(step, q_block, k_t, v_ones, scores_0, scores_1)
    mixed = mixed.astype(bf16)
    for p in range(BLOCK // ROWS):
        out[table[step * (BLOCK // ROWS) + p]] = mixed[p * ROWS : (p + 1) * ROWS]


def encode_kernel(attn, tokens, w_out, gain, bias, w_cross, encoded, cross_kv):
    joined = jnp.concatenate([attn[p] for p in range(SEQ)], axis=1)
    residual = tokens[...].astype(f32) + dot(joined, w_out[...])
    center = residual - jnp.mean(residual, -1, keepdims=True)
    spread = jnp.mean(center * center, -1, keepdims=True)
    state = (center * lax.rsqrt(spread + 1e-05) * gain[...] + bias[...]).astype(bf16)
    encoded[...] = state
    for g in range(SEQ // 2):
        for part in range(2):
            start = part * MODEL + 2 * g * PAIR
            both = dot(state, w_cross[:, start : start + 2 * PAIR]).astype(bf16)
            for p in range(2):
                cross_kv[2 * g + p, :, part * PAIR : (part + 1) * PAIR] = both[
                    :, p * PAIR : (p + 1) * PAIR
                ]


def cross_kernel(place, queries, kv, keep, send, k_t, v_ones, scores_0, scores_1):
    step = pl.program_id(0)

    def q_block(i):
        return queries[pl.ds(pl.multiple_of(i * BLOCK, BLOCK), BLOCK), :]

    @pl.when(step == 0)
    def _():
        k_t[...] = kv[:, :PAIR].T
        v_ones[:, :PAIR] = kv[:, PAIR:]
        v_ones[:, PAIR:] = jnp.ones_like(v_ones[:, PAIR:])
        scores_0[...] = head_scores(q_block(0), k_t[...], 0)

    mixed, total, peak = softmax_pair(step, q_block, k_t, v_ones, scores_0, scores_1)
    weight = peak * score_scale + jnp.log(total)
    is_even = place[1] % 2 == 0
    for g in range(BLOCK // (2 * OWN)):
        even = slice(2 * g * OWN, (2 * g + 1) * OWN)
        odd = slice((2 * g + 1) * OWN, (2 * g + 2) * OWN)
        rows = slice(g * OWN, (g + 1) * OWN)
        for lanes, value in ((slice(0, PAIR), mixed), (slice(PAIR, 2 * PAIR), weight)):
            keep[rows, lanes] = jnp.where(is_even, value[even], value[odd])
            send[rows, lanes] = jnp.where(is_even, value[odd], value[even])


def merge_kernel(keep, received, out):
    here, there = keep[:, PAIR:], received[:, PAIR:]
    top = jnp.maximum(here, there)
    scale_here, scale_there = jnp.exp(here - top), jnp.exp(there - top)
    total = scale_here + scale_there
    mixed = (keep[:, :PAIR] * scale_here + received[:, :PAIR] * scale_there) / total
    weight = top + jnp.log(total)
    high = weight.astype(bf16)
    rest = weight - high.astype(f32)
    middle = rest.astype(bf16)
    low = (rest - middle.astype(f32)).astype(bf16)
    part = lax.broadcasted_iota(jnp.int32, weight.shape, 1) % DH // STAT_LANES
    out[:, :PAIR] = mixed.astype(bf16)
    out[:, PAIR:] = jnp.where(part == 0, high, jnp.where(part == 1, middle, low))


def finish_kernel(parts, out):
    stat = parts[:, :, PAIR:].astype(f32)
    low = lane_low(stat.shape)
    columns = []
    for h in range(2):
        high, middle, rest = (
            stat[:, :, h * DH + p * STAT_LANES : h * DH + p * STAT_LANES + 1] for p in range(3)
        )
        columns.append(high + (middle + rest))
    weight = jnp.where(low, columns[0], columns[1])
    scale = jnp.exp(weight - jnp.max(weight, axis=0, keepdims=True))
    mixed = jnp.sum(parts[:, :, :PAIR].astype(f32) * scale, axis=0) / jnp.sum(scale, axis=0)
    out[...] = jnp.broadcast_to(mixed.astype(bf16)[None], out.shape)


def per_device(tokens, w_qkv, w_out, w_cross, ln_gain, ln_bias, queries):
    seq_index = lax.axis_index("seq")
    span_index = lax.axis_index("span")
    y, x_lo = seq_index // 2, seq_index % 2

    half = ROWS // 2
    peer, up, down = across(tokens), from_below(tokens), from_above(tokens)
    mine = jnp.concatenate(
        [
            lax.dynamic_slice_in_dim(w_qkv, part * MODEL + seq_index * PAIR, PAIR, 1)
            for part in range(3)
        ],
        axis=1,
    )
    mine = jnp.concatenate([mine, along_z(mine, -1), along_z(mine, 1)])
    peer, up, down, mine = lax.optimization_barrier((peer, up, down, mine))
    up_far, down_far = from_below(up[:half]), from_above(down[half:])
    mine = jnp.concatenate([mine, along_z(mine, -3), along_z(mine[: 2 * 32], 3)])
    peer, mine, up_far, down_far = lax.optimization_barrier((peer, mine, up_far, down_far))
    near = (up, down, up_far, down_far)
    side = (across(up_far), across(down_far))
    mine = jnp.concatenate([mine, permute(mine, "span", SPAN, lambda i: i ^ 16)])
    mine, *side = lax.optimization_barrier((mine, *side))
    far = (from_below(peer), from_above(peer), *side)
    twin = permute(mine, "span", SPAN, lambda i: i ^ 1)

    def whole(shape):
        return pl.BlockSpec(shape, lambda *_: (0,) * len(shape))

    place = jnp.stack([seq_index, span_index]).astype(jnp.int32)
    early_rows = 5 * ROWS
    early, weight = pl.pallas_call(
        project_kernel,
        in_specs=[pl.BlockSpec(memory_space=pltpu.SMEM)] + [pl.BlockSpec(memory_space=pltpu.VMEM)] * 8,
        out_shape=[
            jax.ShapeDtypeStruct((early_rows, 3 * PAIR), bf16),
            jax.ShapeDtypeStruct((MODEL, 3 * PAIR), bf16),
        ],
        compiler_params=params(),
        cost_estimate=pl.CostEstimate(
            flops=2 * early_rows * MODEL * 3 * PAIR, bytes_accessed=4 << 20, transcendentals=0
        ),
    )(place, tokens, peer, *near, mine, twin)

    order = jnp.stack(
        [((y + dy) % 4) * 2 + (x_lo ^ flip) for dy, flip in
         ((0, 0), (0, 1), (3, 0), (1, 0), (2, 0), (3, 1), (1, 1), (2, 1))]
    ).astype(jnp.int32)
    length = SEQ * ROWS
    attn = pl.pallas_call(
        attend_kernel,
        grid_spec=pltpu.PrefetchScalarGridSpec(
            num_scalar_prefetch=1,
            grid=(length // BLOCK,),
            in_specs=[
                whole((early_rows, 3 * PAIR)),
                whole((ROWS, MODEL)),
                whole((ROWS, MODEL)),
                whole((ROWS // 2, MODEL)),
                whole((ROWS // 2, MODEL)),
                whole((MODEL, 3 * PAIR)),
            ],
            out_specs=whole((SEQ, ROWS, PAIR)),
            scratch_shapes=[
                pltpu.VMEM((length, PAIR), bf16),
                pltpu.VMEM((PAIR, length), bf16),
                pltpu.VMEM((length, 2 * PAIR), bf16),
                pltpu.VMEM((BLOCK, length), f32),
                pltpu.VMEM((BLOCK, length), f32),
            ],
        ),
        out_shape=jax.ShapeDtypeStruct((SEQ, ROWS, PAIR), bf16),
        compiler_params=params(),
        cost_estimate=pl.CostEstimate(
            flops=8 * length * length * 2 * PAIR, bytes_accessed=4 << 20,
            transcendentals=2 * length * length,
        ),
    )(order, early, *far, weight)
    attn = lax.all_to_all(attn, "seq", split_axis=0, concat_axis=0, tiled=True)

    encoded, cross_kv = pl.pallas_call(
        encode_kernel,
        out_shape=[
            jax.ShapeDtypeStruct((ROWS, MODEL), bf16),
            jax.ShapeDtypeStruct((SEQ, ROWS, 2 * PAIR), bf16),
        ],
        compiler_params=params(),
        cost_estimate=pl.CostEstimate(
            flops=2 * ROWS * MODEL * 3 * MODEL, bytes_accessed=8 << 20, transcendentals=0
        ),
    )(attn, tokens, w_out, ln_gain[None], ln_bias[None], w_cross)

    kv = lax.all_to_all(cross_kv, "seq", split_axis=0, concat_axis=0, tiled=True)
    kv = kv.reshape(length, 2 * PAIR)

    blocks = NQ // BLOCK
    keep, send = pl.pallas_call(
        cross_kernel,
        grid_spec=pltpu.PrefetchScalarGridSpec(
            num_scalar_prefetch=1,
            grid=(blocks,),
            in_specs=[
                pl.BlockSpec((NQ, PAIR), lambda b, place: (0, place[0])),
                whole((length, 2 * PAIR)),
            ],
            out_specs=[
                pl.BlockSpec((BLOCK // 2, 2 * PAIR), lambda b, place: (b, 0)),
                pl.BlockSpec((BLOCK // 2, 2 * PAIR), lambda b, place: (b, 0)),
            ],
            scratch_shapes=[
                pltpu.VMEM((PAIR, length), bf16),
                pltpu.VMEM((length, 2 * PAIR), bf16),
                pltpu.VMEM((BLOCK, length), f32),
                pltpu.VMEM((BLOCK, length), f32),
            ],
        ),
        out_shape=[jax.ShapeDtypeStruct((NQ // 2, 2 * PAIR), f32)] * 2,
        compiler_params=params(),
        cost_estimate=pl.CostEstimate(
            flops=8 * NQ * length * 2 * PAIR, bytes_accessed=2 << 20,
            transcendentals=2 * NQ * length,
        ),
    )(place, queries, kv)

    received = permute(send, "span", SPAN, lambda i: i ^ 1)
    merged = pl.pallas_call(
        merge_kernel,
        out_shape=jax.ShapeDtypeStruct((NQ // 2, 2 * PAIR), bf16),
        compiler_params=params(),
    )(keep, received)
    parts = lax.all_to_all(
        merged.reshape(16, OWN, 2 * PAIR),
        "span",
        split_axis=0,
        concat_axis=0,
        tiled=True,
        axis_index_groups=[list(range(0, SPAN, 2)), list(range(1, SPAN, 2))],
    )
    mine = pl.pallas_call(
        finish_kernel,
        out_shape=jax.ShapeDtypeStruct((SEQ, OWN, PAIR), bf16),
        compiler_params=params(),
    )(parts)
    heads = lax.all_to_all(mine, "seq", split_axis=0, concat_axis=0, tiled=True)
    cross_out = jnp.transpose(heads, (1, 0, 2)).reshape(OWN, MODEL)
    return encoded, cross_out


def solution(mesh):
    in_specs = (P(("span", "seq"), None), P("span", None), P(), P(), P(), P(), P())
    out_specs = (P(("span", "seq"), None), P("span", None))
    return jax.shard_map(
        per_device, mesh=mesh, in_specs=in_specs, out_specs=out_specs, check_vma=False
    )
```

```python
import functools
import math

import jax
import jax.numpy as jnp
from jax import lax
from jax.experimental import pallas as pl
from jax.experimental.pallas import tpu as pltpu
from jax.sharding import PartitionSpec as P

H = 16
DH = 64
PAIR = 2 * DH
MODEL = 1024
ROWS = 256
SEQ = 8
SPAN = 32
OWN = 32
NQ = 1024
STAT_LANES = 16
BLOCK = 512
score_scale = 0.125
LOG2E = math.log2(math.e)
EXP2_SCALE = score_scale * LOG2E

bf16 = jnp.bfloat16
f32 = jnp.float32


def dot(a, b):
    return jnp.dot(a, b, preferred_element_type=f32)


def params(mib=48):
    return pltpu.CompilerParams(vmem_limit_bytes=mib * 1024 * 1024)


def permute(x, axis, size, target):
    return lax.ppermute(x, axis, [(i, target(i)) for i in range(size)])


def lane_low(shape):
    return lax.broadcasted_iota(jnp.int32, shape, len(shape) - 1) < DH


def along_z(block):
    groups = {}
    for i in range(SPAN):
        groups.setdefault((i // 16, i % 2), []).append(i)
    ring = lax.all_to_all(
        jnp.broadcast_to(block[None], (8,) + block.shape),
        "span",
        split_axis=0,
        concat_axis=0,
        tiled=True,
        axis_index_groups=list(groups.values()),
    )
    return ring.reshape(8 * block.shape[0], block.shape[1])


def from_below(x):
    return permute(x, "seq", SEQ, lambda i: (i + 2) % SEQ)


def from_above(x):
    return permute(x, "seq", SEQ, lambda i: (i - 2) % SEQ)


def across(x):
    return permute(x, "seq", SEQ, lambda i: i ^ 1)


def project_kernel(place, own, peer, up, down, up_far, down_far, mine, twin, out, w):
    for k in range(16):
        for core, blocks in enumerate((mine, twin)):
            block = (place[1] & 17) ^ (k // 8 * 16 + core) | k % 8 * 2
            start = pl.multiple_of(block * 32, 32)
            w[pl.ds(start, 32), :] = blocks[k * 32 : (k + 1) * 32, :]
    row = 0
    for piece in (own, peer, up, down, up_far, down_far):
        count = piece.shape[0]
        out[row : row + count, :] = dot(piece[...], w[...]).astype(bf16)
        row += count


def head_scores(q, k_t, head):
    low = lane_low(q.shape)
    zero = jnp.zeros_like(q)
    return dot(jnp.where(low, q, zero) if head == 0 else jnp.where(low, zero, q), k_t)


def weigh(scores, v_ones):
    top = jnp.max(scores, axis=-1, keepdims=True)
    probs = jnp.exp2((scores - top) * EXP2_SCALE).astype(bf16)
    return dot(probs, v_ones), top


def softmax_pair(step, q_block, k_t, v_ones, scores_0, scores_1):
    scores_1[...] = head_scores(q_block(step), k_t[...], 1)
    mixed_0, peak_0 = weigh(scores_0[...], v_ones[...])
    after = jnp.minimum(step + 1, pl.num_programs(0) - 1)
    scores_0[...] = head_scores(q_block(after), k_t[...], 0)
    mixed_1, peak_1 = weigh(scores_1[...], v_ones[...])
    low = lane_low((scores_0.shape[0], PAIR))
    total = jnp.where(low, mixed_0[:, PAIR:], mixed_1[:, PAIR:])
    mixed = jnp.where(low, mixed_0[:, :PAIR], mixed_1[:, :PAIR]) / total
    return mixed, total, jnp.where(low, peak_0, peak_1)


def attend_kernel(
    table, early, up, down, up_far, down_far, w, out, q_all, k_t, v_ones, scores_0, scores_1
):
    step = pl.program_id(0)

    def q_block(i):
        return q_all[pl.ds(pl.multiple_of(i * BLOCK, BLOCK), BLOCK), :]

    @pl.when(step == 0)
    def _():
        v_ones[:, PAIR:] = jnp.ones_like(v_ones[:, PAIR:])
        done = early.shape[0]
        q_all[:done, :] = early[:, :PAIR]
        k_t[:, :done] = early[:, PAIR : 2 * PAIR].T
        v_ones[:done, :PAIR] = early[:, 2 * PAIR :]
        row = done
        for piece in (up, down, up_far, down_far):
            count = piece.shape[0]
            block = dot(piece[...], w[...]).astype(bf16)
            q_all[row : row + count, :] = block[:, :PAIR]
            k_t[:, row : row + count] = block[:, PAIR : 2 * PAIR].T
            v_ones[row : row + count, :PAIR] = block[:, 2 * PAIR :]
            row += count
        scores_0[...] = head_scores(q_block(0), k_t[...], 0)

    mixed, _, _ = softmax_pair(step, q_block, k_t, v_ones, scores_0, scores_1)
    mixed = mixed.astype(bf16)
    for p in range(BLOCK // ROWS):
        out[table[step * (BLOCK // ROWS) + p]] = mixed[p * ROWS : (p + 1) * ROWS]


def encode_kernel(attn, tokens, w_out, gain, bias, w_cross, encoded, cross_kv):
    joined = jnp.concatenate([attn[p] for p in range(SEQ)], axis=1)
    residual = tokens[...].astype(f32) + dot(joined, w_out[...])
    center = residual - jnp.mean(residual, -1, keepdims=True)
    spread = jnp.mean(center * center, -1, keepdims=True)
    state = (center * lax.rsqrt(spread + 1e-05) * gain[...] + bias[...]).astype(bf16)
    encoded[...] = state
    for g in range(SEQ // 2):
        for part in range(2):
            start = part * MODEL + 2 * g * PAIR
            both = dot(state, w_cross[:, start : start + 2 * PAIR]).astype(bf16)
            for p in range(2):
                cross_kv[2 * g + p, :, part * PAIR : (part + 1) * PAIR] = both[
                    :, p * PAIR : (p + 1) * PAIR
                ]


def cross_kernel(place, queries, kv, keep, send, k_t, v_ones, scores_0, scores_1):
    step = pl.program_id(0)

    def q_block(i):
        return queries[pl.ds(pl.multiple_of(i * BLOCK, BLOCK), BLOCK), :]

    @pl.when(step == 0)
    def _():
        k_t[...] = kv[:, :PAIR].T
        v_ones[:, :PAIR] = kv[:, PAIR:]
        v_ones[:, PAIR:] = jnp.ones_like(v_ones[:, PAIR:])
        scores_0[...] = head_scores(q_block(0), k_t[...], 0)

    mixed, total, peak = softmax_pair(step, q_block, k_t, v_ones, scores_0, scores_1)
    weight = peak * score_scale + jnp.log(total)
    is_even = place[1] % 2 == 0
    for g in range(BLOCK // (2 * OWN)):
        even = slice(2 * g * OWN, (2 * g + 1) * OWN)
        odd = slice((2 * g + 1) * OWN, (2 * g + 2) * OWN)
        rows = slice(g * OWN, (g + 1) * OWN)
        for lanes, value in ((slice(0, PAIR), mixed), (slice(PAIR, 2 * PAIR), weight)):
            keep[rows, lanes] = jnp.where(is_even, value[even], value[odd])
            send[rows, lanes] = jnp.where(is_even, value[odd], value[even])


def merge_kernel(keep, received, out):
    here, there = keep[:, PAIR:], received[:, PAIR:]
    top = jnp.maximum(here, there)
    scale_here, scale_there = jnp.exp(here - top), jnp.exp(there - top)
    total = scale_here + scale_there
    mixed = (keep[:, :PAIR] * scale_here + received[:, :PAIR] * scale_there) / total
    weight = top + jnp.log(total)
    high = weight.astype(bf16)
    rest = weight - high.astype(f32)
    middle = rest.astype(bf16)
    low = (rest - middle.astype(f32)).astype(bf16)
    part = lax.broadcasted_iota(jnp.int32, weight.shape, 1) % DH // STAT_LANES
    out[:, :PAIR] = mixed.astype(bf16)
    out[:, PAIR:] = jnp.where(part == 0, high, jnp.where(part == 1, middle, low))


def finish_kernel(parts, out):
    stat = parts[:, :, PAIR:].astype(f32)
    low = lane_low(stat.shape)
    columns = []
    for h in range(2):
        high, middle, rest = (
            stat[:, :, h * DH + p * STAT_LANES : h * DH + p * STAT_LANES + 1] for p in range(3)
        )
        columns.append(high + (middle + rest))
    weight = jnp.where(low, columns[0], columns[1])
    scale = jnp.exp(weight - jnp.max(weight, axis=0, keepdims=True))
    mixed = jnp.sum(parts[:, :, :PAIR].astype(f32) * scale, axis=0) / jnp.sum(scale, axis=0)
    out[...] = jnp.broadcast_to(mixed.astype(bf16)[None], out.shape)


def per_device(tokens, w_qkv, w_out, w_cross, ln_gain, ln_bias, queries):
    seq_index = lax.axis_index("seq")
    span_index = lax.axis_index("span")
    y, x_lo = seq_index // 2, seq_index % 2

    half = ROWS // 2
    peer, up, down = across(tokens), from_below(tokens), from_above(tokens)
    mine = jnp.concatenate(
        [
            lax.dynamic_slice_in_dim(w_qkv, part * MODEL + seq_index * PAIR, PAIR, 1)
            for part in range(3)
        ],
        axis=1,
    )
    mine = along_z(mine)
    peer, up, down, mine = lax.optimization_barrier((peer, up, down, mine))
    up_far, down_far = from_below(up[:half]), from_above(down[half:])
    mine = jnp.concatenate([mine, permute(mine, "span", SPAN, lambda i: i ^ 16)])
    peer, mine, up_far, down_far = lax.optimization_barrier((peer, mine, up_far, down_far))
    near = (up, down, up_far, down_far)
    far = (from_below(peer), from_above(peer), across(up_far), across(down_far))
    twin = permute(mine, "span", SPAN, lambda i: i ^ 1)

    def whole(shape):
        return pl.BlockSpec(shape, lambda *_: (0,) * len(shape))

    place = jnp.stack([seq_index, span_index]).astype(jnp.int32)
    early_rows = 5 * ROWS
    early, weight = pl.pallas_call(
        project_kernel,
        in_specs=[pl.BlockSpec(memory_space=pltpu.SMEM)] + [pl.BlockSpec(memory_space=pltpu.VMEM)] * 8,
        out_shape=[
            jax.ShapeDtypeStruct((early_rows, 3 * PAIR), bf16),
            jax.ShapeDtypeStruct((MODEL, 3 * PAIR), bf16),
        ],
        compiler_params=params(),
        cost_estimate=pl.CostEstimate(
            flops=2 * early_rows * MODEL * 3 * PAIR, bytes_accessed=4 << 20, transcendentals=0
        ),
    )(place, tokens, peer, *near, mine, twin)

    order = jnp.stack(
        [((y + dy) % 4) * 2 + (x_lo ^ flip) for dy, flip in
         ((0, 0), (0, 1), (3, 0), (1, 0), (2, 0), (3, 1), (1, 1), (2, 1))]
    ).astype(jnp.int32)
    length = SEQ * ROWS
    attn = pl.pallas_call(
        attend_kernel,
        grid_spec=pltpu.PrefetchScalarGridSpec(
            num_scalar_prefetch=1,
            grid=(length // BLOCK,),
            in_specs=[
                whole((early_rows, 3 * PAIR)),
                whole((ROWS, MODEL)),
                whole((ROWS, MODEL)),
                whole((ROWS // 2, MODEL)),
                whole((ROWS // 2, MODEL)),
                whole((MODEL, 3 * PAIR)),
            ],
            out_specs=whole((SEQ, ROWS, PAIR)),
            scratch_shapes=[
                pltpu.VMEM((length, PAIR), bf16),
                pltpu.VMEM((PAIR, length), bf16),
                pltpu.VMEM((length, 2 * PAIR), bf16),
                pltpu.VMEM((BLOCK, length), f32),
                pltpu.VMEM((BLOCK, length), f32),
            ],
        ),
        out_shape=jax.ShapeDtypeStruct((SEQ, ROWS, PAIR), bf16),
        compiler_params=params(),
        cost_estimate=pl.CostEstimate(
            flops=8 * length * length * 2 * PAIR, bytes_accessed=4 << 20,
            transcendentals=2 * length * length,
        ),
    )(order, early, *far, weight)
    attn = lax.all_to_all(attn, "seq", split_axis=0, concat_axis=0, tiled=True)

    encoded, cross_kv = pl.pallas_call(
        encode_kernel,
        out_shape=[
            jax.ShapeDtypeStruct((ROWS, MODEL), bf16),
            jax.ShapeDtypeStruct((SEQ, ROWS, 2 * PAIR), bf16),
        ],
        compiler_params=params(),
        cost_estimate=pl.CostEstimate(
            flops=2 * ROWS * MODEL * 3 * MODEL, bytes_accessed=8 << 20, transcendentals=0
        ),
    )(attn, tokens, w_out, ln_gain[None], ln_bias[None], w_cross)

    kv = lax.all_to_all(cross_kv, "seq", split_axis=0, concat_axis=0, tiled=True)
    kv = kv.reshape(length, 2 * PAIR)

    blocks = NQ // BLOCK
    keep, send = pl.pallas_call(
        cross_kernel,
        grid_spec=pltpu.PrefetchScalarGridSpec(
            num_scalar_prefetch=1,
            grid=(blocks,),
            in_specs=[
                pl.BlockSpec((NQ, PAIR), lambda b, place: (0, place[0])),
                whole((length, 2 * PAIR)),
            ],
            out_specs=[
                pl.BlockSpec((BLOCK // 2, 2 * PAIR), lambda b, place: (b, 0)),
                pl.BlockSpec((BLOCK // 2, 2 * PAIR), lambda b, place: (b, 0)),
            ],
            scratch_shapes=[
                pltpu.VMEM((PAIR, length), bf16),
                pltpu.VMEM((length, 2 * PAIR), bf16),
                pltpu.VMEM((BLOCK, length), f32),
                pltpu.VMEM((BLOCK, length), f32),
            ],
        ),
        out_shape=[jax.ShapeDtypeStruct((NQ // 2, 2 * PAIR), f32)] * 2,
        compiler_params=params(),
        cost_estimate=pl.CostEstimate(
            flops=8 * NQ * length * 2 * PAIR, bytes_accessed=2 << 20,
            transcendentals=2 * NQ * length,
        ),
    )(place, queries, kv)

    received = permute(send, "span", SPAN, lambda i: i ^ 1)
    merged = pl.pallas_call(
        merge_kernel,
        out_shape=jax.ShapeDtypeStruct((NQ // 2, 2 * PAIR), bf16),
        compiler_params=params(),
    )(keep, received)
    parts = lax.all_to_all(
        merged.reshape(16, OWN, 2 * PAIR),
        "span",
        split_axis=0,
        concat_axis=0,
        tiled=True,
        axis_index_groups=[list(range(0, SPAN, 2)), list(range(1, SPAN, 2))],
    )
    mine = pl.pallas_call(
        finish_kernel,
        out_shape=jax.ShapeDtypeStruct((SEQ, OWN, PAIR), bf16),
        compiler_params=params(),
    )(parts)
    heads = lax.all_to_all(mine, "seq", split_axis=0, concat_axis=0, tiled=True)
    cross_out = jnp.transpose(heads, (1, 0, 2)).reshape(OWN, MODEL)
    return encoded, cross_out


def solution(mesh):
    in_specs = (P(("span", "seq"), None), P("span", None), P(), P(), P(), P(), P())
    out_specs = (P(("span", "seq"), None), P("span", None))
    return jax.shard_map(
        per_device, mesh=mesh, in_specs=in_specs, out_specs=out_specs, check_vma=False
    )
```

```python
import functools
import math

import jax
import jax.numpy as jnp
from jax import lax
from jax.experimental import pallas as pl
from jax.experimental.pallas import tpu as pltpu
from jax.sharding import PartitionSpec as P

H = 16
DH = 64
PAIR = 2 * DH
MODEL = 1024
ROWS = 256
SEQ = 8
SPAN = 32
OWN = 32
NQ = 1024
STAT_LANES = 16
BLOCK = 512
SPREAD = (8, 4, 2, 16)
NEAR, FAR = 5 * ROWS, 3 * ROWS
NEAR_BLOCK, FAR_BLOCK = 640, 384
FAR_PIECES = 4
score_scale = 0.125
LOG2E = math.log2(math.e)
EXP2_SCALE = score_scale * LOG2E

bf16 = jnp.bfloat16
f32 = jnp.float32


def dot(a, b):
    return jnp.dot(a, b, preferred_element_type=f32)


def params(mib=48):
    return pltpu.CompilerParams(vmem_limit_bytes=mib * 1024 * 1024)


def permute(x, axis, size, target):
    return lax.ppermute(x, axis, [(i, target(i)) for i in range(size)])


def lane_low(shape):
    return lax.broadcasted_iota(jnp.int32, shape, len(shape) - 1) < DH


def spread(blocks, bits):
    flips = (bits[0], bits[1], bits[0] | bits[1])
    return jnp.concatenate([blocks] + [permute(blocks, "span", SPAN, lambda i, f=f: i ^ f) for f in flips])


def from_below(x):
    return permute(x, "seq", SEQ, lambda i: (i + 2) % SEQ)


def from_above(x):
    return permute(x, "seq", SEQ, lambda i: (i - 2) % SEQ)


def across(x):
    return permute(x, "seq", SEQ, lambda i: i ^ 1)


def head_scores(q, k_t, head):
    low = lane_low(q.shape)
    zero = jnp.zeros_like(q)
    return dot(jnp.where(low, q, zero) if head == 0 else jnp.where(low, zero, q), k_t)


def weigh(scores, v_ones):
    top = jnp.max(scores, axis=-1, keepdims=True)
    probs = jnp.exp2((scores - top) * EXP2_SCALE).astype(bf16)
    return dot(probs, v_ones), top


def softmax_pair(step, steps, q_block, k_t, v_ones, scores_0, scores_1):
    scores_1[...] = head_scores(q_block(step), k_t[...], 1)
    mixed_0, peak_0 = weigh(scores_0[...], v_ones[...])
    scores_0[...] = head_scores(q_block(jnp.minimum(step + 1, steps - 1)), k_t[...], 0)
    mixed_1, peak_1 = weigh(scores_1[...], v_ones[...])
    low = lane_low((scores_0.shape[0], PAIR))
    total = jnp.where(low, mixed_0[:, PAIR:], mixed_1[:, PAIR:])
    mixed = jnp.where(low, mixed_0[:, :PAIR], mixed_1[:, :PAIR]) / total
    return mixed, jnp.where(low, peak_0, peak_1) * score_scale + jnp.log(total)


def merge_pair(mixed_a, weight_a, mixed_b, weight_b):
    top = jnp.maximum(weight_a, weight_b)
    scale_a, scale_b = jnp.exp(weight_a - top), jnp.exp(weight_b - top)
    total = scale_a + scale_b
    return (mixed_a * scale_a + mixed_b * scale_b) / total, top + jnp.log(total)


def project(pieces, w, q_all, k_t, v_ones, row):
    for piece in pieces:
        count = piece.shape[0]
        block = dot(piece[...], w[...]).astype(bf16)
        q_all[row : row + count, :] = block[:, :PAIR]
        k_t[:, row : row + count] = block[:, PAIR : 2 * PAIR].T
        v_ones[row : row + count, :PAIR] = block[:, 2 * PAIR :]
        row += count
    v_ones[:, PAIR:] = jnp.ones_like(v_ones[:, PAIR:])


def row_block(q_all, size, start=0):
    return lambda i: q_all[pl.ds(pl.multiple_of(start + i * size, 128), size), :]


def near_kernel(
    place, own, peer, up, down, up_far, down_far, mine, twin,
    q_all, k_t, v_ones, w, mixed, weight, scores_0, scores_1,
):
    step = pl.program_id(0)
    q_block = row_block(q_all, NEAR_BLOCK)

    @pl.when(step == 0)
    def _():
        for k in range(1 << len(SPREAD)):
            flip = sum(bit for p, bit in enumerate(SPREAD) if k >> p & 1)
            for core, blocks in enumerate((mine, twin)):
                start = pl.multiple_of((place[1] ^ (flip + core)) * 32, 32)
                w[pl.ds(start, 32), :] = blocks[k * 32 : (k + 1) * 32, :]
        project((own, peer, up, down, up_far, down_far), w, q_all, k_t, v_ones, 0)
        scores_0[...] = head_scores(q_block(0), k_t[...], 0)

    mixed[...], weight[...] = softmax_pair(
        step, NEAR // NEAR_BLOCK, q_block, k_t, v_ones, scores_0, scores_1
    )


def far_kernel(table, *refs):
    pieces, rest = refs[:FAR_PIECES], refs[FAR_PIECES:]
    w, q_near, k_near, v_near, mixed_near, weight_near, out = rest[:7]
    q_far, k_far, v_far, k_t, v_ones, near_0, near_1, far_0, far_1 = rest[7:]
    step = pl.program_id(0)
    near_steps, far_steps = NEAR // NEAR_BLOCK, FAR // FAR_BLOCK
    near_rows, far_rows = row_block(q_near, NEAR_BLOCK), row_block(q_far, FAR_BLOCK)

    def store(mixed, first):
        for c in range(mixed.shape[0] // 128):
            g = first // 128 + c
            start = pl.multiple_of(g % 2 * 128, 128)
            out[table[g // 2], pl.ds(start, 128), :] = mixed[c * 128 : (c + 1) * 128].astype(bf16)

    @pl.when(step == 0)
    def _():
        project(pieces, w, q_far, k_far, v_far, 0)
        k_t[:, :NEAR] = k_near[...]
        k_t[:, NEAR:] = k_far[...]
        v_ones[:NEAR, :] = v_near[...]
        v_ones[NEAR:, :] = v_far[...]
        near_0[...] = head_scores(near_rows(0), k_far[...], 0)

    @pl.when(step < near_steps)
    def _():
        mixed, weight = softmax_pair(step, near_steps, near_rows, k_far, v_far, near_0, near_1)
        rows = pl.ds(pl.multiple_of(step * NEAR_BLOCK, 128), NEAR_BLOCK)
        mixed, _ = merge_pair(mixed, weight, mixed_near[rows, :], weight_near[rows, :])
        store(mixed, step * NEAR_BLOCK)

    @pl.when(step == near_steps)
    def _():
        far_0[...] = head_scores(far_rows(0), k_t[...], 0)

    @pl.when(step >= near_steps)
    def _():
        mixed, _ = softmax_pair(step - near_steps, far_steps, far_rows, k_t, v_ones, far_0, far_1)
        store(mixed, NEAR + (step - near_steps) * FAR_BLOCK)


def encode_kernel(
    attn, tokens, w_out, gain, bias, w_cross_far, encoded, cross_kv, w_cross, arrived
):
    fetch = pltpu.make_async_copy(w_cross_far, w_cross, arrived)
    fetch.start()
    joined = jnp.concatenate([attn[p] for p in range(SEQ)], axis=1)
    residual = tokens[...].astype(f32) + dot(joined, w_out[...])
    center = residual - jnp.mean(residual, -1, keepdims=True)
    spread = jnp.mean(center * center, -1, keepdims=True)
    state = (center * lax.rsqrt(spread + 1e-05) * gain[...] + bias[...]).astype(bf16)
    encoded[...] = state
    fetch.wait()
    for g in range(SEQ // 2):
        for part in range(2):
            start = part * MODEL + 2 * g * PAIR
            both = dot(state, w_cross[:, start : start + 2 * PAIR]).astype(bf16)
            for p in range(2):
                cross_kv[2 * g + p, :, part * PAIR : (part + 1) * PAIR] = both[
                    :, p * PAIR : (p + 1) * PAIR
                ]


def cross_kernel(place, queries, kv, keep, send, k_t, v_ones, scores_0, scores_1):
    step = pl.program_id(0)
    q_block = row_block(queries, BLOCK)

    @pl.when(step == 0)
    def _():
        k_t[...] = kv[:, :PAIR].T
        v_ones[:, :PAIR] = kv[:, PAIR:]
        v_ones[:, PAIR:] = jnp.ones_like(v_ones[:, PAIR:])
        scores_0[...] = head_scores(q_block(0), k_t[...], 0)

    mixed, weight = softmax_pair(
        step, NQ // BLOCK, q_block, k_t, v_ones, scores_0, scores_1
    )
    is_even = place[1] % 2 == 0
    for g in range(BLOCK // (2 * OWN)):
        even = slice(2 * g * OWN, (2 * g + 1) * OWN)
        odd = slice((2 * g + 1) * OWN, (2 * g + 2) * OWN)
        rows = slice(g * OWN, (g + 1) * OWN)
        for lanes, value in ((slice(0, PAIR), mixed), (slice(PAIR, 2 * PAIR), weight)):
            keep[rows, lanes] = jnp.where(is_even, value[even], value[odd])
            send[rows, lanes] = jnp.where(is_even, value[odd], value[even])


def merge_kernel(keep, received, out):
    mixed, weight = merge_pair(keep[:, :PAIR], keep[:, PAIR:], received[:, :PAIR], received[:, PAIR:])
    high = weight.astype(bf16)
    rest = weight - high.astype(f32)
    middle = rest.astype(bf16)
    low = (rest - middle.astype(f32)).astype(bf16)
    part = lax.broadcasted_iota(jnp.int32, weight.shape, 1) % DH // STAT_LANES
    out[:, :PAIR] = mixed.astype(bf16)
    out[:, PAIR:] = jnp.where(part == 0, high, jnp.where(part == 1, middle, low))


def finish_kernel(parts, out):
    stat = parts[:, :, PAIR:].astype(f32)
    low = lane_low(stat.shape)
    columns = []
    for h in range(2):
        high, middle, rest = (
            stat[:, :, h * DH + p * STAT_LANES : h * DH + p * STAT_LANES + 1] for p in range(3)
        )
        columns.append(high + (middle + rest))
    weight = jnp.where(low, columns[0], columns[1])
    scale = jnp.exp(weight - jnp.max(weight, axis=0, keepdims=True))
    mixed = jnp.sum(parts[:, :, :PAIR].astype(f32) * scale, axis=0) / jnp.sum(scale, axis=0)
    out[...] = jnp.broadcast_to(mixed.astype(bf16)[None], out.shape)


def per_device(tokens, w_qkv, w_out, w_cross, ln_gain, ln_bias, queries):
    seq_index = lax.axis_index("seq")
    span_index = lax.axis_index("span")
    y, x_lo = seq_index // 2, seq_index % 2

    half = ROWS // 2
    peer, up, down = across(tokens), from_below(tokens), from_above(tokens)
    mine = jnp.concatenate(
        [
            lax.dynamic_slice_in_dim(w_qkv, part * MODEL + seq_index * PAIR, PAIR, 1)
            for part in range(3)
        ],
        axis=1,
    )
    mine = spread(mine, SPREAD[:2])
    peer, up, down, mine = lax.optimization_barrier((peer, up, down, mine))
    near = (up, down, from_below(up[:half]), from_above(down[half:]))
    mine = spread(mine, SPREAD[2:])
    peer, mine = lax.optimization_barrier((peer, mine))
    far = (from_below(peer), from_above(peer), across(near[2]), across(near[3]))
    twin = permute(mine, "span", SPAN, lambda i: i ^ 1)

    def whole(shape):
        return pl.BlockSpec(shape, lambda *_: (0,) * len(shape))

    place = jnp.stack([seq_index, span_index]).astype(jnp.int32)
    length = SEQ * ROWS
    shapes = [
        jax.ShapeDtypeStruct((NEAR, PAIR), bf16),
        jax.ShapeDtypeStruct((PAIR, NEAR), bf16),
        jax.ShapeDtypeStruct((NEAR, 2 * PAIR), bf16),
        jax.ShapeDtypeStruct((MODEL, 3 * PAIR), bf16),
        jax.ShapeDtypeStruct((NEAR, PAIR), f32),
        jax.ShapeDtypeStruct((NEAR, PAIR), f32),
    ]
    pieces = (tokens, peer, *near, mine, twin)
    q_near, k_near, v_near, weight, mixed_near, weight_near = pl.pallas_call(
        near_kernel,
        grid=(NEAR // NEAR_BLOCK,),
        in_specs=[pl.BlockSpec(memory_space=pltpu.SMEM)] + [whole(p.shape) for p in pieces],
        out_specs=[whole(p.shape) for p in shapes[:4]]
        + [pl.BlockSpec((NEAR_BLOCK, PAIR), lambda b: (b, 0))] * 2,
        out_shape=shapes,
        scratch_shapes=[pltpu.VMEM((NEAR_BLOCK, NEAR), f32)] * 2,
        compiler_params=params(28),
        cost_estimate=pl.CostEstimate(
            flops=2 * NEAR * MODEL * 3 * PAIR, bytes_accessed=4 << 20, transcendentals=0
        ),
    )(place, *pieces)

    order = jnp.stack(
        [((y + dy) % 4) * 2 + (x_lo ^ flip) for dy, flip in
         ((0, 0), (0, 1), (3, 0), (1, 0), (2, 0), (3, 1), (1, 1), (2, 1))]
    ).astype(jnp.int32)
    operands = (*far, weight, q_near, k_near, v_near, mixed_near, weight_near)
    attn = pl.pallas_call(
        far_kernel,
        grid_spec=pltpu.PrefetchScalarGridSpec(
            num_scalar_prefetch=1,
            grid=(NEAR // NEAR_BLOCK + FAR // FAR_BLOCK,),
            in_specs=[whole(p.shape) for p in operands],
            out_specs=whole((SEQ, ROWS, PAIR)),
            scratch_shapes=[
                pltpu.VMEM((FAR, PAIR), bf16),
                pltpu.VMEM((PAIR, FAR), bf16),
                pltpu.VMEM((FAR, 2 * PAIR), bf16),
                pltpu.VMEM((PAIR, length), bf16),
                pltpu.VMEM((length, 2 * PAIR), bf16),
                pltpu.VMEM((NEAR_BLOCK, FAR), f32),
                pltpu.VMEM((NEAR_BLOCK, FAR), f32),
                pltpu.VMEM((FAR_BLOCK, length), f32),
                pltpu.VMEM((FAR_BLOCK, length), f32),
            ],
        ),
        out_shape=jax.ShapeDtypeStruct((SEQ, ROWS, PAIR), bf16),
        compiler_params=params(32),
        cost_estimate=pl.CostEstimate(
            flops=6 * length * length * 2 * PAIR, bytes_accessed=4 << 20,
            transcendentals=2 * length * length,
        ),
    )(order, *operands)
    attn = lax.all_to_all(attn, "seq", split_axis=0, concat_axis=0, tiled=True)

    encoded, cross_kv = pl.pallas_call(
        encode_kernel,
        in_specs=[pl.BlockSpec(memory_space=pltpu.VMEM)] * 5 + [pl.BlockSpec(memory_space=pl.ANY)],
        scratch_shapes=[pltpu.VMEM((MODEL, 2 * MODEL), bf16), pltpu.SemaphoreType.DMA],
        out_shape=[
            jax.ShapeDtypeStruct((ROWS, MODEL), bf16),
            jax.ShapeDtypeStruct((SEQ, ROWS, 2 * PAIR), bf16),
        ],
        compiler_params=params(),
        cost_estimate=pl.CostEstimate(
            flops=2 * ROWS * MODEL * 3 * MODEL, bytes_accessed=8 << 20, transcendentals=0
        ),
    )(attn, tokens, w_out, ln_gain[None], ln_bias[None], w_cross)

    kv = lax.all_to_all(cross_kv, "seq", split_axis=0, concat_axis=0, tiled=True)
    kv = kv.reshape(length, 2 * PAIR)

    blocks = NQ // BLOCK
    keep, send = pl.pallas_call(
        cross_kernel,
        grid_spec=pltpu.PrefetchScalarGridSpec(
            num_scalar_prefetch=1,
            grid=(blocks,),
            in_specs=[
                pl.BlockSpec((NQ, PAIR), lambda b, place: (0, place[0])),
                whole((length, 2 * PAIR)),
            ],
            out_specs=[
                pl.BlockSpec((BLOCK // 2, 2 * PAIR), lambda b, place: (b, 0)),
                pl.BlockSpec((BLOCK // 2, 2 * PAIR), lambda b, place: (b, 0)),
            ],
            scratch_shapes=[
                pltpu.VMEM((PAIR, length), bf16),
                pltpu.VMEM((length, 2 * PAIR), bf16),
                pltpu.VMEM((BLOCK, length), f32),
                pltpu.VMEM((BLOCK, length), f32),
            ],
        ),
        out_shape=[jax.ShapeDtypeStruct((NQ // 2, 2 * PAIR), f32)] * 2,
        compiler_params=params(),
        cost_estimate=pl.CostEstimate(
            flops=8 * NQ * length * 2 * PAIR, bytes_accessed=2 << 20,
            transcendentals=2 * NQ * length,
        ),
    )(place, queries, kv)

    received = permute(send, "span", SPAN, lambda i: i ^ 1)
    merged = pl.pallas_call(
        merge_kernel,
        out_shape=jax.ShapeDtypeStruct((NQ // 2, 2 * PAIR), bf16),
        compiler_params=params(),
    )(keep, received)
    parts = lax.all_to_all(
        merged.reshape(16, OWN, 2 * PAIR),
        "span",
        split_axis=0,
        concat_axis=0,
        tiled=True,
        axis_index_groups=[list(range(0, SPAN, 2)), list(range(1, SPAN, 2))],
    )
    mine = pl.pallas_call(
        finish_kernel,
        out_shape=jax.ShapeDtypeStruct((SEQ, OWN, PAIR), bf16),
        compiler_params=params(),
    )(parts)
    heads = lax.all_to_all(mine, "seq", split_axis=0, concat_axis=0, tiled=True)
    cross_out = jnp.transpose(heads, (1, 0, 2)).reshape(OWN, MODEL)
    return encoded, cross_out


def solution(mesh):
    in_specs = (P(("span", "seq"), None), P("span", None), P(), P(), P(), P(), P())
    out_specs = (P(("span", "seq"), None), P("span", None))
    return jax.shard_map(
        per_device, mesh=mesh, in_specs=in_specs, out_specs=out_specs, check_vma=False
    )
```

```python
import functools
import math

import jax
import jax.numpy as jnp
from jax import lax
from jax.experimental import pallas as pl
from jax.experimental.pallas import tpu as pltpu
from jax.sharding import PartitionSpec as P

H = 16
DH = 64
PAIR = 2 * DH
MODEL = 1024
ROWS = 256
SEQ = 8
SPAN = 32
OWN = 32
NQ = 1024
STAT_LANES = 16
BLOCK = 512
SPREAD = (2, 4, 8, 16)
NEAR, FAR = 5 * ROWS, 3 * ROWS
NEAR_BLOCK, FAR_BLOCK = 640, 384
FAR_PIECES = 4
score_scale = 0.125
LOG2E = math.log2(math.e)
EXP2_SCALE = score_scale * LOG2E

bf16 = jnp.bfloat16
f32 = jnp.float32


def dot(a, b):
    return jnp.dot(a, b, preferred_element_type=f32)


def params(mib=48):
    return pltpu.CompilerParams(vmem_limit_bytes=mib * 1024 * 1024)


def permute(x, axis, size, target):
    return lax.ppermute(x, axis, [(i, target(i)) for i in range(size)])


def lane_low(shape):
    return lax.broadcasted_iota(jnp.int32, shape, len(shape) - 1) < DH


def spread(blocks, bits):
    flips = (bits[0], bits[1], bits[0] | bits[1])
    return jnp.concatenate([blocks] + [permute(blocks, "span", SPAN, lambda i, f=f: i ^ f) for f in flips])


def from_below(x):
    return permute(x, "seq", SEQ, lambda i: (i + 2) % SEQ)


def from_above(x):
    return permute(x, "seq", SEQ, lambda i: (i - 2) % SEQ)


def across(x):
    return permute(x, "seq", SEQ, lambda i: i ^ 1)


def head_scores(q, k_t, head):
    low = lane_low(q.shape)
    zero = jnp.zeros_like(q)
    return dot(jnp.where(low, q, zero) if head == 0 else jnp.where(low, zero, q), k_t)


def weigh(scores, v_ones):
    top = jnp.max(scores, axis=-1, keepdims=True)
    probs = jnp.exp2((scores - top) * EXP2_SCALE).astype(bf16)
    return dot(probs, v_ones), top


def softmax_pair(step, steps, q_block, k_t, v_ones, scores_0, scores_1):
    scores_1[...] = head_scores(q_block(step), k_t[...], 1)
    mixed_0, peak_0 = weigh(scores_0[...], v_ones[...])
    scores_0[...] = head_scores(q_block(jnp.minimum(step + 1, steps - 1)), k_t[...], 0)
    mixed_1, peak_1 = weigh(scores_1[...], v_ones[...])
    low = lane_low((scores_0.shape[0], PAIR))
    total = jnp.where(low, mixed_0[:, PAIR:], mixed_1[:, PAIR:])
    mixed = jnp.where(low, mixed_0[:, :PAIR], mixed_1[:, :PAIR]) / total
    return mixed, jnp.where(low, peak_0, peak_1) * score_scale + jnp.log(total)


def merge_pair(mixed_a, weight_a, mixed_b, weight_b):
    top = jnp.maximum(weight_a, weight_b)
    scale_a, scale_b = jnp.exp(weight_a - top), jnp.exp(weight_b - top)
    total = scale_a + scale_b
    return (mixed_a * scale_a + mixed_b * scale_b) / total, top + jnp.log(total)


def project(pieces, w, q_all, k_t, v_ones, row):
    for piece in pieces:
        count = piece.shape[0]
        block = dot(piece[...], w[...]).astype(bf16)
        q_all[row : row + count, :] = block[:, :PAIR]
        k_t[:, row : row + count] = block[:, PAIR : 2 * PAIR].T
        v_ones[row : row + count, :PAIR] = block[:, 2 * PAIR :]
        row += count
    v_ones[:, PAIR:] = jnp.ones_like(v_ones[:, PAIR:])


def row_block(q_all, size, start=0):
    return lambda i: q_all[pl.ds(pl.multiple_of(start + i * size, 128), size), :]


def near_kernel(
    place, own, peer, up, down, up_far, down_far, mine, twin,
    q_all, k_t, v_ones, w, mixed, weight, scores_0, scores_1,
):
    step = pl.program_id(0)
    q_block = row_block(q_all, NEAR_BLOCK)

    @pl.when(step == 0)
    def _():
        for k in range(1 << len(SPREAD)):
            flip = sum(bit for p, bit in enumerate(SPREAD) if k >> p & 1)
            for core, blocks in enumerate((mine, twin)):
                start = pl.multiple_of((place[1] ^ (flip + core)) * 32, 32)
                w[pl.ds(start, 32), :] = blocks[k * 32 : (k + 1) * 32, :]
        project((own, peer, up, down, up_far, down_far), w, q_all, k_t, v_ones, 0)
        scores_0[...] = head_scores(q_block(0), k_t[...], 0)

    mixed[...], weight[...] = softmax_pair(
        step, NEAR // NEAR_BLOCK, q_block, k_t, v_ones, scores_0, scores_1
    )


def far_kernel(table, *refs):
    pieces, rest = refs[:FAR_PIECES], refs[FAR_PIECES:]
    w, q_near, k_near, v_near, mixed_near, weight_near, out = rest[:7]
    q_far, k_far, v_far, k_t, v_ones, near_0, near_1, far_0, far_1 = rest[7:]
    step = pl.program_id(0)
    near_steps, far_steps = NEAR // NEAR_BLOCK, FAR // FAR_BLOCK
    near_rows, far_rows = row_block(q_near, NEAR_BLOCK), row_block(q_far, FAR_BLOCK)

    def store(mixed, first):
        for c in range(mixed.shape[0] // 128):
            g = first // 128 + c
            start = pl.multiple_of(g % 2 * 128, 128)
            out[table[g // 2], pl.ds(start, 128), :] = mixed[c * 128 : (c + 1) * 128].astype(bf16)

    @pl.when(step == 0)
    def _():
        project(pieces, w, q_far, k_far, v_far, 0)
        k_t[:, :NEAR] = k_near[...]
        k_t[:, NEAR:] = k_far[...]
        v_ones[:NEAR, :] = v_near[...]
        v_ones[NEAR:, :] = v_far[...]
        near_0[...] = head_scores(near_rows(0), k_far[...], 0)

    @pl.when(step < near_steps)
    def _():
        mixed, weight = softmax_pair(step, near_steps, near_rows, k_far, v_far, near_0, near_1)
        rows = pl.ds(pl.multiple_of(step * NEAR_BLOCK, 128), NEAR_BLOCK)
        mixed, _ = merge_pair(mixed, weight, mixed_near[rows, :], weight_near[rows, :])
        store(mixed, step * NEAR_BLOCK)

    @pl.when(step == near_steps)
    def _():
        far_0[...] = head_scores(far_rows(0), k_t[...], 0)

    @pl.when(step >= near_steps)
    def _():
        mixed, _ = softmax_pair(step - near_steps, far_steps, far_rows, k_t, v_ones, far_0, far_1)
        store(mixed, NEAR + (step - near_steps) * FAR_BLOCK)


def encode_kernel(
    attn, tokens, w_out, gain, bias, w_cross_far, encoded, cross_kv, w_cross, arrived
):
    fetch = pltpu.make_async_copy(w_cross_far, w_cross, arrived)
    fetch.start()
    joined = jnp.concatenate([attn[p] for p in range(SEQ)], axis=1)
    residual = tokens[...].astype(f32) + dot(joined, w_out[...])
    center = residual - jnp.mean(residual, -1, keepdims=True)
    spread = jnp.mean(center * center, -1, keepdims=True)
    state = (center * lax.rsqrt(spread + 1e-05) * gain[...] + bias[...]).astype(bf16)
    encoded[...] = state
    fetch.wait()
    for g in range(SEQ // 2):
        for part in range(2):
            start = part * MODEL + 2 * g * PAIR
            both = dot(state, w_cross[:, start : start + 2 * PAIR]).astype(bf16)
            for p in range(2):
                cross_kv[2 * g + p, :, part * PAIR : (part + 1) * PAIR] = both[
                    :, p * PAIR : (p + 1) * PAIR
                ]


def cross_kernel(place, queries, kv, keep, send, k_t, v_ones, scores_0, scores_1):
    step = pl.program_id(0)
    q_block = row_block(queries, BLOCK)

    @pl.when(step == 0)
    def _():
        k_t[...] = kv[:, :PAIR].T
        v_ones[:, :PAIR] = kv[:, PAIR:]
        v_ones[:, PAIR:] = jnp.ones_like(v_ones[:, PAIR:])
        scores_0[...] = head_scores(q_block(0), k_t[...], 0)

    mixed, weight = softmax_pair(
        step, NQ // BLOCK, q_block, k_t, v_ones, scores_0, scores_1
    )
    is_even = place[1] % 2 == 0
    for g in range(BLOCK // (2 * OWN)):
        even = slice(2 * g * OWN, (2 * g + 1) * OWN)
        odd = slice((2 * g + 1) * OWN, (2 * g + 2) * OWN)
        rows = slice(g * OWN, (g + 1) * OWN)
        for lanes, value in ((slice(0, PAIR), mixed), (slice(PAIR, 2 * PAIR), weight)):
            keep[rows, lanes] = jnp.where(is_even, value[even], value[odd])
            send[rows, lanes] = jnp.where(is_even, value[odd], value[even])


def merge_kernel(keep, received, out):
    mixed, weight = merge_pair(keep[:, :PAIR], keep[:, PAIR:], received[:, :PAIR], received[:, PAIR:])
    high = weight.astype(bf16)
    rest = weight - high.astype(f32)
    middle = rest.astype(bf16)
    low = (rest - middle.astype(f32)).astype(bf16)
    part = lax.broadcasted_iota(jnp.int32, weight.shape, 1) % DH // STAT_LANES
    out[:, :PAIR] = mixed.astype(bf16)
    out[:, PAIR:] = jnp.where(part == 0, high, jnp.where(part == 1, middle, low))


def finish_kernel(parts, out):
    stat = parts[:, :, PAIR:].astype(f32)
    low = lane_low(stat.shape)
    columns = []
    for h in range(2):
        high, middle, rest = (
            stat[:, :, h * DH + p * STAT_LANES : h * DH + p * STAT_LANES + 1] for p in range(3)
        )
        columns.append(high + (middle + rest))
    weight = jnp.where(low, columns[0], columns[1])
    scale = jnp.exp(weight - jnp.max(weight, axis=0, keepdims=True))
    mixed = jnp.sum(parts[:, :, :PAIR].astype(f32) * scale, axis=0) / jnp.sum(scale, axis=0)
    out[...] = jnp.broadcast_to(mixed.astype(bf16)[None], out.shape)


def per_device(tokens, w_qkv, w_out, w_cross, ln_gain, ln_bias, queries):
    seq_index = lax.axis_index("seq")
    span_index = lax.axis_index("span")
    y, x_lo = seq_index // 2, seq_index % 2

    half = ROWS // 2
    peer, up, down = across(tokens), from_below(tokens), from_above(tokens)
    mine = jnp.concatenate(
        [
            lax.dynamic_slice_in_dim(w_qkv, part * MODEL + seq_index * PAIR, PAIR, 1)
            for part in range(3)
        ],
        axis=1,
    )
    for bit in SPREAD[:2]:
        mine = jnp.concatenate([mine, permute(mine, "span", SPAN, lambda i, f=bit: i ^ f)])
    peer, up, down, mine = lax.optimization_barrier((peer, up, down, mine))
    near = (up, down, from_below(up[:half]), from_above(down[half:]))
    mine = spread(mine, SPREAD[2:])
    peer, mine = lax.optimization_barrier((peer, mine))
    far = (from_below(peer), from_above(peer), across(near[2]), across(near[3]))
    twin = permute(mine, "span", SPAN, lambda i: i ^ 1)

    def whole(shape):
        return pl.BlockSpec(shape, lambda *_: (0,) * len(shape))

    place = jnp.stack([seq_index, span_index]).astype(jnp.int32)
    length = SEQ * ROWS
    shapes = [
        jax.ShapeDtypeStruct((NEAR, PAIR), bf16),
        jax.ShapeDtypeStruct((PAIR, NEAR), bf16),
        jax.ShapeDtypeStruct((NEAR, 2 * PAIR), bf16),
        jax.ShapeDtypeStruct((MODEL, 3 * PAIR), bf16),
        jax.ShapeDtypeStruct((NEAR, PAIR), f32),
        jax.ShapeDtypeStruct((NEAR, PAIR), f32),
    ]
    pieces = (tokens, peer, *near, mine, twin)
    q_near, k_near, v_near, weight, mixed_near, weight_near = pl.pallas_call(
        near_kernel,
        grid=(NEAR // NEAR_BLOCK,),
        in_specs=[pl.BlockSpec(memory_space=pltpu.SMEM)] + [whole(p.shape) for p in pieces],
        out_specs=[whole(p.shape) for p in shapes[:4]]
        + [pl.BlockSpec((NEAR_BLOCK, PAIR), lambda b: (b, 0))] * 2,
        out_shape=shapes,
        scratch_shapes=[pltpu.VMEM((NEAR_BLOCK, NEAR), f32)] * 2,
        compiler_params=params(28),
        cost_estimate=pl.CostEstimate(
            flops=2 * NEAR * MODEL * 3 * PAIR, bytes_accessed=4 << 20, transcendentals=0
        ),
    )(place, *pieces)

    order = jnp.stack(
        [((y + dy) % 4) * 2 + (x_lo ^ flip) for dy, flip in
         ((0, 0), (0, 1), (3, 0), (1, 0), (2, 0), (3, 1), (1, 1), (2, 1))]
    ).astype(jnp.int32)
    operands = (*far, weight, q_near, k_near, v_near, mixed_near, weight_near)
    attn = pl.pallas_call(
        far_kernel,
        grid_spec=pltpu.PrefetchScalarGridSpec(
            num_scalar_prefetch=1,
            grid=(NEAR // NEAR_BLOCK + FAR // FAR_BLOCK,),
            in_specs=[whole(p.shape) for p in operands],
            out_specs=whole((SEQ, ROWS, PAIR)),
            scratch_shapes=[
                pltpu.VMEM((FAR, PAIR), bf16),
                pltpu.VMEM((PAIR, FAR), bf16),
                pltpu.VMEM((FAR, 2 * PAIR), bf16),
                pltpu.VMEM((PAIR, length), bf16),
                pltpu.VMEM((length, 2 * PAIR), bf16),
                pltpu.VMEM((NEAR_BLOCK, FAR), f32),
                pltpu.VMEM((NEAR_BLOCK, FAR), f32),
                pltpu.VMEM((FAR_BLOCK, length), f32),
                pltpu.VMEM((FAR_BLOCK, length), f32),
            ],
        ),
        out_shape=jax.ShapeDtypeStruct((SEQ, ROWS, PAIR), bf16),
        compiler_params=params(32),
        cost_estimate=pl.CostEstimate(
            flops=6 * length * length * 2 * PAIR, bytes_accessed=4 << 20,
            transcendentals=2 * length * length,
        ),
    )(order, *operands)
    attn = lax.all_to_all(attn, "seq", split_axis=0, concat_axis=0, tiled=True)

    encoded, cross_kv = pl.pallas_call(
        encode_kernel,
        in_specs=[pl.BlockSpec(memory_space=pltpu.VMEM)] * 5 + [pl.BlockSpec(memory_space=pl.ANY)],
        scratch_shapes=[pltpu.VMEM((MODEL, 2 * MODEL), bf16), pltpu.SemaphoreType.DMA],
        out_shape=[
            jax.ShapeDtypeStruct((ROWS, MODEL), bf16),
            jax.ShapeDtypeStruct((SEQ, ROWS, 2 * PAIR), bf16),
        ],
        compiler_params=params(),
        cost_estimate=pl.CostEstimate(
            flops=2 * ROWS * MODEL * 3 * MODEL, bytes_accessed=8 << 20, transcendentals=0
        ),
    )(attn, tokens, w_out, ln_gain[None], ln_bias[None], w_cross)

    kv = lax.all_to_all(cross_kv, "seq", split_axis=0, concat_axis=0, tiled=True)
    kv = kv.reshape(length, 2 * PAIR)

    blocks = NQ // BLOCK
    keep, send = pl.pallas_call(
        cross_kernel,
        grid_spec=pltpu.PrefetchScalarGridSpec(
            num_scalar_prefetch=1,
            grid=(blocks,),
            in_specs=[
                pl.BlockSpec((NQ, PAIR), lambda b, place: (0, place[0])),
                whole((length, 2 * PAIR)),
            ],
            out_specs=[
                pl.BlockSpec((BLOCK // 2, 2 * PAIR), lambda b, place: (b, 0)),
                pl.BlockSpec((BLOCK // 2, 2 * PAIR), lambda b, place: (b, 0)),
            ],
            scratch_shapes=[
                pltpu.VMEM((PAIR, length), bf16),
                pltpu.VMEM((length, 2 * PAIR), bf16),
                pltpu.VMEM((BLOCK, length), f32),
                pltpu.VMEM((BLOCK, length), f32),
            ],
        ),
        out_shape=[jax.ShapeDtypeStruct((NQ // 2, 2 * PAIR), f32)] * 2,
        compiler_params=params(),
        cost_estimate=pl.CostEstimate(
            flops=8 * NQ * length * 2 * PAIR, bytes_accessed=2 << 20,
            transcendentals=2 * NQ * length,
        ),
    )(place, queries, kv)

    received = permute(send, "span", SPAN, lambda i: i ^ 1)
    merged = pl.pallas_call(
        merge_kernel,
        out_shape=jax.ShapeDtypeStruct((NQ // 2, 2 * PAIR), bf16),
        compiler_params=params(),
    )(keep, received)
    parts = lax.all_to_all(
        merged.reshape(16, OWN, 2 * PAIR),
        "span",
        split_axis=0,
        concat_axis=0,
        tiled=True,
        axis_index_groups=[list(range(0, SPAN, 2)), list(range(1, SPAN, 2))],
    )
    mine = pl.pallas_call(
        finish_kernel,
        out_shape=jax.ShapeDtypeStruct((SEQ, OWN, PAIR), bf16),
        compiler_params=params(),
    )(parts)
    heads = lax.all_to_all(mine, "seq", split_axis=0, concat_axis=0, tiled=True)
    cross_out = jnp.transpose(heads, (1, 0, 2)).reshape(OWN, MODEL)
    return encoded, cross_out


def solution(mesh):
    in_specs = (P(("span", "seq"), None), P("span", None), P(), P(), P(), P(), P())
    out_specs = (P(("span", "seq"), None), P("span", None))
    return jax.shard_map(
        per_device, mesh=mesh, in_specs=in_specs, out_specs=out_specs, check_vma=False
    )
```

```python
import functools
import math

import jax
import jax.numpy as jnp
from jax import lax
from jax.experimental import pallas as pl
from jax.experimental.pallas import tpu as pltpu
from jax.sharding import PartitionSpec as P

H = 16
DH = 64
PAIR = 2 * DH
MODEL = 1024
ROWS = 256
SEQ = 8
SPAN = 32
OWN = 32
NQ = 1024
STAT_LANES = 16
BLOCK = 512
SPREAD = (4, 8, 2, 16)
NEAR, FAR = 5 * ROWS, 3 * ROWS
NEAR_BLOCK, FAR_BLOCK = 640, 384
FAR_PIECES = 4
score_scale = 0.125
LOG2E = math.log2(math.e)
EXP2_SCALE = score_scale * LOG2E

bf16 = jnp.bfloat16
f32 = jnp.float32


def dot(a, b):
    return jnp.dot(a, b, preferred_element_type=f32)


def params(mib=48):
    return pltpu.CompilerParams(vmem_limit_bytes=mib * 1024 * 1024)


def permute(x, axis, size, target):
    return lax.ppermute(x, axis, [(i, target(i)) for i in range(size)])


def lane_low(shape):
    return lax.broadcasted_iota(jnp.int32, shape, len(shape) - 1) < DH


def spread(blocks, bits):
    flips = (bits[0], bits[1], bits[0] | bits[1])
    return jnp.concatenate([blocks] + [permute(blocks, "span", SPAN, lambda i, f=f: i ^ f) for f in flips])


def from_below(x):
    return permute(x, "seq", SEQ, lambda i: (i + 2) % SEQ)


def from_above(x):
    return permute(x, "seq", SEQ, lambda i: (i - 2) % SEQ)


def across(x):
    return permute(x, "seq", SEQ, lambda i: i ^ 1)


def head_scores(q, k_t, head):
    low = lane_low(q.shape)
    zero = jnp.zeros_like(q)
    return dot(jnp.where(low, q, zero) if head == 0 else jnp.where(low, zero, q), k_t)


def weigh(scores, v_ones):
    top = jnp.max(scores, axis=-1, keepdims=True)
    probs = jnp.exp2((scores - top) * EXP2_SCALE).astype(bf16)
    return dot(probs, v_ones), top


def softmax_pair(step, steps, q_block, k_t, v_ones, scores_0, scores_1):
    scores_1[...] = head_scores(q_block(step), k_t[...], 1)
    mixed_0, peak_0 = weigh(scores_0[...], v_ones[...])
    scores_0[...] = head_scores(q_block(jnp.minimum(step + 1, steps - 1)), k_t[...], 0)
    mixed_1, peak_1 = weigh(scores_1[...], v_ones[...])
    low = lane_low((scores_0.shape[0], PAIR))
    total = jnp.where(low, mixed_0[:, PAIR:], mixed_1[:, PAIR:])
    mixed = jnp.where(low, mixed_0[:, :PAIR], mixed_1[:, :PAIR]) / total
    return mixed, jnp.where(low, peak_0, peak_1) * score_scale + jnp.log(total)


def merge_pair(mixed_a, weight_a, mixed_b, weight_b):
    top = jnp.maximum(weight_a, weight_b)
    scale_a, scale_b = jnp.exp(weight_a - top), jnp.exp(weight_b - top)
    total = scale_a + scale_b
    return (mixed_a * scale_a + mixed_b * scale_b) / total, top + jnp.log(total)


def project(pieces, w, q_all, k_t, v_ones, row):
    for piece in pieces:
        count = piece.shape[0]
        block = dot(piece[...], w[...]).astype(bf16)
        q_all[row : row + count, :] = block[:, :PAIR]
        k_t[:, row : row + count] = block[:, PAIR : 2 * PAIR].T
        v_ones[row : row + count, :PAIR] = block[:, 2 * PAIR :]
        row += count
    v_ones[:, PAIR:] = jnp.ones_like(v_ones[:, PAIR:])


def row_block(q_all, size, start=0):
    return lambda i: q_all[pl.ds(pl.multiple_of(start + i * size, 128), size), :]


def near_kernel(
    place, own, peer, up, down, up_far, down_far, mine, twin,
    q_all, k_t, v_ones, w, mixed, weight, scores_0, scores_1,
):
    step = pl.program_id(0)
    q_block = row_block(q_all, NEAR_BLOCK)

    @pl.when(step == 0)
    def _():
        for k in range(1 << len(SPREAD)):
            flip = sum(bit for p, bit in enumerate(SPREAD) if k >> p & 1)
            for core, blocks in enumerate((mine, twin)):
                start = pl.multiple_of((place[1] ^ (flip + core)) * 32, 32)
                w[pl.ds(start, 32), :] = blocks[k * 32 : (k + 1) * 32, :]
        project((own, peer, up, down, up_far, down_far), w, q_all, k_t, v_ones, 0)
        scores_0[...] = head_scores(q_block(0), k_t[...], 0)

    mixed[...], weight[...] = softmax_pair(
        step, NEAR // NEAR_BLOCK, q_block, k_t, v_ones, scores_0, scores_1
    )


def far_kernel(table, *refs):
    pieces, rest = refs[:FAR_PIECES], refs[FAR_PIECES:]
    w, q_near, k_near, v_near, mixed_near, weight_near, out = rest[:7]
    q_far, k_far, v_far, k_t, v_ones, near_0, near_1, far_0, far_1 = rest[7:]
    step = pl.program_id(0)
    near_steps, far_steps = NEAR // NEAR_BLOCK, FAR // FAR_BLOCK
    near_rows, far_rows = row_block(q_near, NEAR_BLOCK), row_block(q_far, FAR_BLOCK)

    def store(mixed, first):
        for c in range(mixed.shape[0] // 128):
            g = first // 128 + c
            start = pl.multiple_of(g % 2 * 128, 128)
            out[table[g // 2], pl.ds(start, 128), :] = mixed[c * 128 : (c + 1) * 128].astype(bf16)

    @pl.when(step == 0)
    def _():
        project(pieces, w, q_far, k_far, v_far, 0)
        k_t[:, :NEAR] = k_near[...]
        k_t[:, NEAR:] = k_far[...]
        v_ones[:NEAR, :] = v_near[...]
        v_ones[NEAR:, :] = v_far[...]
        near_0[...] = head_scores(near_rows(0), k_far[...], 0)

    @pl.when(step < near_steps)
    def _():
        mixed, weight = softmax_pair(step, near_steps, near_rows, k_far, v_far, near_0, near_1)
        rows = pl.ds(pl.multiple_of(step * NEAR_BLOCK, 128), NEAR_BLOCK)
        mixed, _ = merge_pair(mixed, weight, mixed_near[rows, :], weight_near[rows, :])
        store(mixed, step * NEAR_BLOCK)

    @pl.when(step == near_steps)
    def _():
        far_0[...] = head_scores(far_rows(0), k_t[...], 0)

    @pl.when(step >= near_steps)
    def _():
        mixed, _ = softmax_pair(step - near_steps, far_steps, far_rows, k_t, v_ones, far_0, far_1)
        store(mixed, NEAR + (step - near_steps) * FAR_BLOCK)


def encode_kernel(
    attn, tokens, w_out, gain, bias, w_cross_far, encoded, cross_kv, w_cross, arrived
):
    fetch = pltpu.make_async_copy(w_cross_far, w_cross, arrived)
    fetch.start()
    joined = jnp.concatenate([attn[p] for p in range(SEQ)], axis=1)
    residual = tokens[...].astype(f32) + dot(joined, w_out[...])
    center = residual - jnp.mean(residual, -1, keepdims=True)
    spread = jnp.mean(center * center, -1, keepdims=True)
    state = (center * lax.rsqrt(spread + 1e-05) * gain[...] + bias[...]).astype(bf16)
    encoded[...] = state
    fetch.wait()
    for g in range(SEQ // 2):
        for part in range(2):
            start = part * MODEL + 2 * g * PAIR
            both = dot(state, w_cross[:, start : start + 2 * PAIR]).astype(bf16)
            for p in range(2):
                cross_kv[2 * g + p, :, part * PAIR : (part + 1) * PAIR] = both[
                    :, p * PAIR : (p + 1) * PAIR
                ]


def cross_kernel(place, queries, kv, keep, send, k_t, v_ones, scores_0, scores_1):
    step = pl.program_id(0)
    q_block = row_block(queries, BLOCK)

    @pl.when(step == 0)
    def _():
        k_t[...] = kv[:, :PAIR].T
        v_ones[:, :PAIR] = kv[:, PAIR:]
        v_ones[:, PAIR:] = jnp.ones_like(v_ones[:, PAIR:])
        scores_0[...] = head_scores(q_block(0), k_t[...], 0)

    mixed, weight = softmax_pair(
        step, NQ // BLOCK, q_block, k_t, v_ones, scores_0, scores_1
    )
    is_even = place[1] % 2 == 0
    for g in range(BLOCK // (2 * OWN)):
        even = slice(2 * g * OWN, (2 * g + 1) * OWN)
        odd = slice((2 * g + 1) * OWN, (2 * g + 2) * OWN)
        rows = slice(g * OWN, (g + 1) * OWN)
        for lanes, value in ((slice(0, PAIR), mixed), (slice(PAIR, 2 * PAIR), weight)):
            keep[rows, lanes] = jnp.where(is_even, value[even], value[odd])
            send[rows, lanes] = jnp.where(is_even, value[odd], value[even])


def merge_kernel(keep, received, out):
    mixed, weight = merge_pair(keep[:, :PAIR], keep[:, PAIR:], received[:, :PAIR], received[:, PAIR:])
    high = weight.astype(bf16)
    rest = weight - high.astype(f32)
    middle = rest.astype(bf16)
    low = (rest - middle.astype(f32)).astype(bf16)
    part = lax.broadcasted_iota(jnp.int32, weight.shape, 1) % DH // STAT_LANES
    out[:, :PAIR] = mixed.astype(bf16)
    out[:, PAIR:] = jnp.where(part == 0, high, jnp.where(part == 1, middle, low))


def finish_kernel(parts, out):
    stat = parts[:, :, PAIR:].astype(f32)
    low = lane_low(stat.shape)
    columns = []
    for h in range(2):
        high, middle, rest = (
            stat[:, :, h * DH + p * STAT_LANES : h * DH + p * STAT_LANES + 1] for p in range(3)
        )
        columns.append(high + (middle + rest))
    weight = jnp.where(low, columns[0], columns[1])
    scale = jnp.exp(weight - jnp.max(weight, axis=0, keepdims=True))
    mixed = jnp.sum(parts[:, :, :PAIR].astype(f32) * scale, axis=0) / jnp.sum(scale, axis=0)
    out[...] = jnp.broadcast_to(mixed.astype(bf16)[None], out.shape)


def per_device(tokens, w_qkv, w_out, w_cross, ln_gain, ln_bias, queries):
    seq_index = lax.axis_index("seq")
    span_index = lax.axis_index("span")
    y, x_lo = seq_index // 2, seq_index % 2

    half = ROWS // 2
    peer, up, down = across(tokens), from_below(tokens), from_above(tokens)
    mine = jnp.concatenate(
        [
            lax.dynamic_slice_in_dim(w_qkv, part * MODEL + seq_index * PAIR, PAIR, 1)
            for part in range(3)
        ],
        axis=1,
    )
    for bit in SPREAD[:2]:
        mine = jnp.concatenate([mine, permute(mine, "span", SPAN, lambda i, f=bit: i ^ f)])
    peer, up, down, mine = lax.optimization_barrier((peer, up, down, mine))
    near = (up, down, from_below(up[:half]), from_above(down[half:]))
    mine = spread(mine, SPREAD[2:])
    peer, mine = lax.optimization_barrier((peer, mine))
    far = (from_below(peer), from_above(peer), across(near[2]), across(near[3]))
    twin = permute(mine, "span", SPAN, lambda i: i ^ 1)

    def whole(shape):
        return pl.BlockSpec(shape, lambda *_: (0,) * len(shape))

    place = jnp.stack([seq_index, span_index]).astype(jnp.int32)
    length = SEQ * ROWS
    shapes = [
        jax.ShapeDtypeStruct((NEAR, PAIR), bf16),
        jax.ShapeDtypeStruct((PAIR, NEAR), bf16),
        jax.ShapeDtypeStruct((NEAR, 2 * PAIR), bf16),
        jax.ShapeDtypeStruct((MODEL, 3 * PAIR), bf16),
        jax.ShapeDtypeStruct((NEAR, PAIR), f32),
        jax.ShapeDtypeStruct((NEAR, PAIR), f32),
    ]
    pieces = (tokens, peer, *near, mine, twin)
    q_near, k_near, v_near, weight, mixed_near, weight_near = pl.pallas_call(
        near_kernel,
        grid=(NEAR // NEAR_BLOCK,),
        in_specs=[pl.BlockSpec(memory_space=pltpu.SMEM)] + [whole(p.shape) for p in pieces],
        out_specs=[whole(p.shape) for p in shapes[:4]]
        + [pl.BlockSpec((NEAR_BLOCK, PAIR), lambda b: (b, 0))] * 2,
        out_shape=shapes,
        scratch_shapes=[pltpu.VMEM((NEAR_BLOCK, NEAR), f32)] * 2,
        compiler_params=params(28),
        cost_estimate=pl.CostEstimate(
            flops=2 * NEAR * MODEL * 3 * PAIR, bytes_accessed=4 << 20, transcendentals=0
        ),
    )(place, *pieces)

    order = jnp.stack(
        [((y + dy) % 4) * 2 + (x_lo ^ flip) for dy, flip in
         ((0, 0), (0, 1), (3, 0), (1, 0), (2, 0), (3, 1), (1, 1), (2, 1))]
    ).astype(jnp.int32)
    operands = (*far, weight, q_near, k_near, v_near, mixed_near, weight_near)
    attn = pl.pallas_call(
        far_kernel,
        grid_spec=pltpu.PrefetchScalarGridSpec(
            num_scalar_prefetch=1,
            grid=(NEAR // NEAR_BLOCK + FAR // FAR_BLOCK,),
            in_specs=[whole(p.shape) for p in operands],
            out_specs=whole((SEQ, ROWS, PAIR)),
            scratch_shapes=[
                pltpu.VMEM((FAR, PAIR), bf16),
                pltpu.VMEM((PAIR, FAR), bf16),
                pltpu.VMEM((FAR, 2 * PAIR), bf16),
                pltpu.VMEM((PAIR, length), bf16),
                pltpu.VMEM((length, 2 * PAIR), bf16),
                pltpu.VMEM((NEAR_BLOCK, FAR), f32),
                pltpu.VMEM((NEAR_BLOCK, FAR), f32),
                pltpu.VMEM((FAR_BLOCK, length), f32),
                pltpu.VMEM((FAR_BLOCK, length), f32),
            ],
        ),
        out_shape=jax.ShapeDtypeStruct((SEQ, ROWS, PAIR), bf16),
        compiler_params=params(32),
        cost_estimate=pl.CostEstimate(
            flops=6 * length * length * 2 * PAIR, bytes_accessed=4 << 20,
            transcendentals=2 * length * length,
        ),
    )(order, *operands)
    attn = lax.all_to_all(attn, "seq", split_axis=0, concat_axis=0, tiled=True)

    encoded, cross_kv = pl.pallas_call(
        encode_kernel,
        in_specs=[pl.BlockSpec(memory_space=pltpu.VMEM)] * 5 + [pl.BlockSpec(memory_space=pl.ANY)],
        scratch_shapes=[pltpu.VMEM((MODEL, 2 * MODEL), bf16), pltpu.SemaphoreType.DMA],
        out_shape=[
            jax.ShapeDtypeStruct((ROWS, MODEL), bf16),
            jax.ShapeDtypeStruct((SEQ, ROWS, 2 * PAIR), bf16),
        ],
        compiler_params=params(),
        cost_estimate=pl.CostEstimate(
            flops=2 * ROWS * MODEL * 3 * MODEL, bytes_accessed=8 << 20, transcendentals=0
        ),
    )(attn, tokens, w_out, ln_gain[None], ln_bias[None], w_cross)

    kv = lax.all_to_all(cross_kv, "seq", split_axis=0, concat_axis=0, tiled=True)
    kv = kv.reshape(length, 2 * PAIR)

    blocks = NQ // BLOCK
    keep, send = pl.pallas_call(
        cross_kernel,
        grid_spec=pltpu.PrefetchScalarGridSpec(
            num_scalar_prefetch=1,
            grid=(blocks,),
            in_specs=[
                pl.BlockSpec((NQ, PAIR), lambda b, place: (0, place[0])),
                whole((length, 2 * PAIR)),
            ],
            out_specs=[
                pl.BlockSpec((BLOCK // 2, 2 * PAIR), lambda b, place: (b, 0)),
                pl.BlockSpec((BLOCK // 2, 2 * PAIR), lambda b, place: (b, 0)),
            ],
            scratch_shapes=[
                pltpu.VMEM((PAIR, length), bf16),
                pltpu.VMEM((length, 2 * PAIR), bf16),
                pltpu.VMEM((BLOCK, length), f32),
                pltpu.VMEM((BLOCK, length), f32),
            ],
        ),
        out_shape=[jax.ShapeDtypeStruct((NQ // 2, 2 * PAIR), f32)] * 2,
        compiler_params=params(),
        cost_estimate=pl.CostEstimate(
            flops=8 * NQ * length * 2 * PAIR, bytes_accessed=2 << 20,
            transcendentals=2 * NQ * length,
        ),
    )(place, queries, kv)

    received = permute(send, "span", SPAN, lambda i: i ^ 1)
    merged = pl.pallas_call(
        merge_kernel,
        out_shape=jax.ShapeDtypeStruct((NQ // 2, 2 * PAIR), bf16),
        compiler_params=params(),
    )(keep, received)
    parts = lax.all_to_all(
        merged.reshape(16, OWN, 2 * PAIR),
        "span",
        split_axis=0,
        concat_axis=0,
        tiled=True,
        axis_index_groups=[list(range(0, SPAN, 2)), list(range(1, SPAN, 2))],
    )
    mine = pl.pallas_call(
        finish_kernel,
        out_shape=jax.ShapeDtypeStruct((SEQ, OWN, PAIR), bf16),
        compiler_params=params(),
    )(parts)
    heads = lax.all_to_all(mine, "seq", split_axis=0, concat_axis=0, tiled=True)
    cross_out = jnp.transpose(heads, (1, 0, 2)).reshape(OWN, MODEL)
    return encoded, cross_out


def solution(mesh):
    in_specs = (P(("span", "seq"), None), P("span", None), P(), P(), P(), P(), P())
    out_specs = (P(("span", "seq"), None), P("span", None))
    return jax.shard_map(
        per_device, mesh=mesh, in_specs=in_specs, out_specs=out_specs, check_vma=False
    )
```

```python
import functools
import math

import jax
import jax.numpy as jnp
from jax import lax
from jax.experimental import pallas as pl
from jax.experimental.pallas import tpu as pltpu
from jax.sharding import PartitionSpec as P

H = 16
DH = 64
PAIR = 2 * DH
MODEL = 1024
ROWS = 256
SEQ = 8
SPAN = 32
OWN = 32
NQ = 1024
STAT_LANES = 16
BLOCK = 512
SPREAD = (4, 8, 2, 16)
NEAR, FAR = 5 * ROWS, 3 * ROWS
NEAR_BLOCK, FAR_BLOCK = 640, 384
FAR_PIECES = 4
score_scale = 0.125
LOG2E = math.log2(math.e)
EXP2_SCALE = score_scale * LOG2E

bf16 = jnp.bfloat16
f32 = jnp.float32


def dot(a, b):
    return jnp.dot(a, b, preferred_element_type=f32)


def params(mib=48):
    return pltpu.CompilerParams(vmem_limit_bytes=mib * 1024 * 1024)


def permute(x, axis, size, target):
    return lax.ppermute(x, axis, [(i, target(i)) for i in range(size)])


def lane_low(shape):
    return lax.broadcasted_iota(jnp.int32, shape, len(shape) - 1) < DH


def spread(blocks, bits):
    flips = (bits[0], bits[1], bits[0] | bits[1])
    return jnp.concatenate([blocks] + [permute(blocks, "span", SPAN, lambda i, f=f: i ^ f) for f in flips])


def from_below(x):
    return permute(x, "seq", SEQ, lambda i: (i + 2) % SEQ)


def from_above(x):
    return permute(x, "seq", SEQ, lambda i: (i - 2) % SEQ)


def across(x):
    return permute(x, "seq", SEQ, lambda i: i ^ 1)


def head_scores(q, k_t, head):
    low = lane_low(q.shape)
    zero = jnp.zeros_like(q)
    return dot(jnp.where(low, q, zero) if head == 0 else jnp.where(low, zero, q), k_t)


def weigh(scores, v_ones):
    top = jnp.max(scores, axis=-1, keepdims=True)
    probs = jnp.exp2((scores - top) * EXP2_SCALE).astype(bf16)
    return dot(probs, v_ones), top


def softmax_pair(step, steps, q_block, k_t, v_ones, scores_0, scores_1):
    scores_1[...] = head_scores(q_block(step), k_t[...], 1)
    mixed_0, peak_0 = weigh(scores_0[...], v_ones[...])
    scores_0[...] = head_scores(q_block(jnp.minimum(step + 1, steps - 1)), k_t[...], 0)
    mixed_1, peak_1 = weigh(scores_1[...], v_ones[...])
    low = lane_low((scores_0.shape[0], PAIR))
    total = jnp.where(low, mixed_0[:, PAIR:], mixed_1[:, PAIR:])
    mixed = jnp.where(low, mixed_0[:, :PAIR], mixed_1[:, :PAIR]) / total
    return mixed, jnp.where(low, peak_0, peak_1) * score_scale + jnp.log(total)


def merge_pair(mixed_a, weight_a, mixed_b, weight_b):
    top = jnp.maximum(weight_a, weight_b)
    scale_a, scale_b = jnp.exp(weight_a - top), jnp.exp(weight_b - top)
    total = scale_a + scale_b
    return (mixed_a * scale_a + mixed_b * scale_b) / total, top + jnp.log(total)


def project(pieces, w, q_all, k_t, v_ones, row):
    for piece in pieces:
        count = piece.shape[0]
        block = dot(piece[...], w[...]).astype(bf16)
        q_all[row : row + count, :] = block[:, :PAIR]
        k_t[:, row : row + count] = block[:, PAIR : 2 * PAIR].T
        v_ones[row : row + count, :PAIR] = block[:, 2 * PAIR :]
        row += count
    v_ones[:, PAIR:] = jnp.ones_like(v_ones[:, PAIR:])


def row_block(q_all, size, start=0):
    return lambda i: q_all[pl.ds(pl.multiple_of(start + i * size, 128), size), :]


def near_kernel(
    place, own, peer, up, down, up_far, down_far, mine, twin,
    q_all, k_t, v_ones, w, mixed, weight, scores_0, scores_1,
):
    step = pl.program_id(0)
    q_block = row_block(q_all, NEAR_BLOCK)

    @pl.when(step == 0)
    def _():
        for k in range(1 << len(SPREAD)):
            flip = sum(bit for p, bit in enumerate(SPREAD) if k >> p & 1)
            for core, blocks in enumerate((mine, twin)):
                start = pl.multiple_of((place[1] ^ (flip + core)) * 32, 32)
                w[pl.ds(start, 32), :] = blocks[k * 32 : (k + 1) * 32, :]
        project((own, peer, up, down, up_far, down_far), w, q_all, k_t, v_ones, 0)
        scores_0[...] = head_scores(q_block(0), k_t[...], 0)

    mixed[...], weight[...] = softmax_pair(
        step, NEAR // NEAR_BLOCK, q_block, k_t, v_ones, scores_0, scores_1
    )


def far_kernel(table, *refs):
    pieces, rest = refs[:FAR_PIECES], refs[FAR_PIECES:]
    w, q_near, k_near, v_near, mixed_near, weight_near, out = rest[:7]
    q_far, k_far, v_far, k_t, v_ones, near_0, near_1, far_0, far_1 = rest[7:]
    step = pl.program_id(0)
    near_steps, far_steps = NEAR // NEAR_BLOCK, FAR // FAR_BLOCK
    near_rows, far_rows = row_block(q_near, NEAR_BLOCK), row_block(q_far, FAR_BLOCK)

    def store(mixed, first):
        for c in range(mixed.shape[0] // 128):
            g = first // 128 + c
            start = pl.multiple_of(g % 2 * 128, 128)
            out[table[g // 2], pl.ds(start, 128), :] = mixed[c * 128 : (c + 1) * 128].astype(bf16)

    @pl.when(step == 0)
    def _():
        project(pieces, w, q_far, k_far, v_far, 0)
        k_t[:, :NEAR] = k_near[...]
        k_t[:, NEAR:] = k_far[...]
        v_ones[:NEAR, :] = v_near[...]
        v_ones[NEAR:, :] = v_far[...]
        near_0[...] = head_scores(near_rows(0), k_far[...], 0)

    @pl.when(step < near_steps)
    def _():
        mixed, weight = softmax_pair(step, near_steps, near_rows, k_far, v_far, near_0, near_1)
        rows = pl.ds(pl.multiple_of(step * NEAR_BLOCK, 128), NEAR_BLOCK)
        mixed, _ = merge_pair(mixed, weight, mixed_near[rows, :], weight_near[rows, :])
        store(mixed, step * NEAR_BLOCK)

    @pl.when(step == near_steps)
    def _():
        far_0[...] = head_scores(far_rows(0), k_t[...], 0)

    @pl.when(step >= near_steps)
    def _():
        mixed, _ = softmax_pair(step - near_steps, far_steps, far_rows, k_t, v_ones, far_0, far_1)
        store(mixed, NEAR + (step - near_steps) * FAR_BLOCK)


def encode_kernel(
    attn, tokens, w_out, gain, bias, w_cross_far, encoded, cross_kv, w_cross, arrived
):
    fetch = pltpu.make_async_copy(w_cross_far, w_cross, arrived)
    fetch.start()
    joined = jnp.concatenate([attn[p] for p in range(SEQ)], axis=1)
    residual = tokens[...].astype(f32) + dot(joined, w_out[...])
    center = residual - jnp.mean(residual, -1, keepdims=True)
    spread = jnp.mean(center * center, -1, keepdims=True)
    state = (center * lax.rsqrt(spread + 1e-05) * gain[...] + bias[...]).astype(bf16)
    encoded[...] = state
    fetch.wait()
    for g in range(SEQ // 2):
        for part in range(2):
            start = part * MODEL + 2 * g * PAIR
            both = dot(state, w_cross[:, start : start + 2 * PAIR]).astype(bf16)
            for p in range(2):
                cross_kv[2 * g + p, :, part * PAIR : (part + 1) * PAIR] = both[
                    :, p * PAIR : (p + 1) * PAIR
                ]


def cross_kernel(place, queries, kv, keep, send, k_t, v_ones, scores_0, scores_1):
    step = pl.program_id(0)
    q_block = row_block(queries, BLOCK)

    @pl.when(step == 0)
    def _():
        k_t[...] = kv[:, :PAIR].T
        v_ones[:, :PAIR] = kv[:, PAIR:]
        v_ones[:, PAIR:] = jnp.ones_like(v_ones[:, PAIR:])
        scores_0[...] = head_scores(q_block(0), k_t[...], 0)

    mixed, weight = softmax_pair(
        step, NQ // BLOCK, q_block, k_t, v_ones, scores_0, scores_1
    )
    is_even = place[1] % 2 == 0
    for g in range(BLOCK // (2 * OWN)):
        even = slice(2 * g * OWN, (2 * g + 1) * OWN)
        odd = slice((2 * g + 1) * OWN, (2 * g + 2) * OWN)
        rows = slice(g * OWN, (g + 1) * OWN)
        for lanes, value in ((slice(0, PAIR), mixed), (slice(PAIR, 2 * PAIR), weight)):
            keep[rows, lanes] = jnp.where(is_even, value[even], value[odd])
            send[rows, lanes] = jnp.where(is_even, value[odd], value[even])


def merge_kernel(keep, received, out):
    mixed, weight = merge_pair(keep[:, :PAIR], keep[:, PAIR:], received[:, :PAIR], received[:, PAIR:])
    high = weight.astype(bf16)
    rest = weight - high.astype(f32)
    middle = rest.astype(bf16)
    low = (rest - middle.astype(f32)).astype(bf16)
    part = lax.broadcasted_iota(jnp.int32, weight.shape, 1) % DH // STAT_LANES
    out[:, :PAIR] = mixed.astype(bf16)
    out[:, PAIR:] = jnp.where(part == 0, high, jnp.where(part == 1, middle, low))


def finish_kernel(parts, out):
    stat = parts[:, :, PAIR:].astype(f32)
    low = lane_low(stat.shape)
    columns = []
    for h in range(2):
        high, middle, rest = (
            stat[:, :, h * DH + p * STAT_LANES : h * DH + p * STAT_LANES + 1] for p in range(3)
        )
        columns.append(high + (middle + rest))
    weight = jnp.where(low, columns[0], columns[1])
    scale = jnp.exp(weight - jnp.max(weight, axis=0, keepdims=True))
    mixed = jnp.sum(parts[:, :, :PAIR].astype(f32) * scale, axis=0) / jnp.sum(scale, axis=0)
    out[...] = jnp.broadcast_to(mixed.astype(bf16)[None], out.shape)


def per_device(tokens, w_qkv, w_out, w_cross, ln_gain, ln_bias, queries):
    seq_index = lax.axis_index("seq")
    span_index = lax.axis_index("span")
    y, x_lo = seq_index // 2, seq_index % 2

    half = ROWS // 2
    peer, up, down = across(tokens), from_below(tokens), from_above(tokens)
    mine = jnp.concatenate(
        [
            lax.dynamic_slice_in_dim(w_qkv, part * MODEL + seq_index * PAIR, PAIR, 1)
            for part in range(3)
        ],
        axis=1,
    )
    for bit in SPREAD[:2]:
        mine = jnp.concatenate([mine, permute(mine, "span", SPAN, lambda i, f=bit: i ^ f)])
    peer, up, down, mine = lax.optimization_barrier((peer, up, down, mine))
    near = (up, down, from_below(up[:half]), from_above(down[half:]))
    mine = spread(mine, SPREAD[2:])

    far = (from_below(peer), from_above(peer), across(near[2]), across(near[3]))
    twin = permute(mine, "span", SPAN, lambda i: i ^ 1)

    def whole(shape):
        return pl.BlockSpec(shape, lambda *_: (0,) * len(shape))

    place = jnp.stack([seq_index, span_index]).astype(jnp.int32)
    length = SEQ * ROWS
    shapes = [
        jax.ShapeDtypeStruct((NEAR, PAIR), bf16),
        jax.ShapeDtypeStruct((PAIR, NEAR), bf16),
        jax.ShapeDtypeStruct((NEAR, 2 * PAIR), bf16),
        jax.ShapeDtypeStruct((MODEL, 3 * PAIR), bf16),
        jax.ShapeDtypeStruct((NEAR, PAIR), f32),
        jax.ShapeDtypeStruct((NEAR, PAIR), f32),
    ]
    pieces = (tokens, peer, *near, mine, twin)
    q_near, k_near, v_near, weight, mixed_near, weight_near = pl.pallas_call(
        near_kernel,
        grid=(NEAR // NEAR_BLOCK,),
        in_specs=[pl.BlockSpec(memory_space=pltpu.SMEM)] + [whole(p.shape) for p in pieces],
        out_specs=[whole(p.shape) for p in shapes[:4]]
        + [pl.BlockSpec((NEAR_BLOCK, PAIR), lambda b: (b, 0))] * 2,
        out_shape=shapes,
        scratch_shapes=[pltpu.VMEM((NEAR_BLOCK, NEAR), f32)] * 2,
        compiler_params=params(28),
        cost_estimate=pl.CostEstimate(
            flops=2 * NEAR * MODEL * 3 * PAIR, bytes_accessed=4 << 20, transcendentals=0
        ),
    )(place, *pieces)

    order = jnp.stack(
        [((y + dy) % 4) * 2 + (x_lo ^ flip) for dy, flip in
         ((0, 0), (0, 1), (3, 0), (1, 0), (2, 0), (3, 1), (1, 1), (2, 1))]
    ).astype(jnp.int32)
    operands = (*far, weight, q_near, k_near, v_near, mixed_near, weight_near)
    attn = pl.pallas_call(
        far_kernel,
        grid_spec=pltpu.PrefetchScalarGridSpec(
            num_scalar_prefetch=1,
            grid=(NEAR // NEAR_BLOCK + FAR // FAR_BLOCK,),
            in_specs=[whole(p.shape) for p in operands],
            out_specs=whole((SEQ, ROWS, PAIR)),
            scratch_shapes=[
                pltpu.VMEM((FAR, PAIR), bf16),
                pltpu.VMEM((PAIR, FAR), bf16),
                pltpu.VMEM((FAR, 2 * PAIR), bf16),
                pltpu.VMEM((PAIR, length), bf16),
                pltpu.VMEM((length, 2 * PAIR), bf16),
                pltpu.VMEM((NEAR_BLOCK, FAR), f32),
                pltpu.VMEM((NEAR_BLOCK, FAR), f32),
                pltpu.VMEM((FAR_BLOCK, length), f32),
                pltpu.VMEM((FAR_BLOCK, length), f32),
            ],
        ),
        out_shape=jax.ShapeDtypeStruct((SEQ, ROWS, PAIR), bf16),
        compiler_params=params(32),
        cost_estimate=pl.CostEstimate(
            flops=6 * length * length * 2 * PAIR, bytes_accessed=4 << 20,
            transcendentals=2 * length * length,
        ),
    )(order, *operands)
    attn = lax.all_to_all(attn, "seq", split_axis=0, concat_axis=0, tiled=True)

    encoded, cross_kv = pl.pallas_call(
        encode_kernel,
        in_specs=[pl.BlockSpec(memory_space=pltpu.VMEM)] * 5 + [pl.BlockSpec(memory_space=pl.ANY)],
        scratch_shapes=[pltpu.VMEM((MODEL, 2 * MODEL), bf16), pltpu.SemaphoreType.DMA],
        out_shape=[
            jax.ShapeDtypeStruct((ROWS, MODEL), bf16),
            jax.ShapeDtypeStruct((SEQ, ROWS, 2 * PAIR), bf16),
        ],
        compiler_params=params(),
        cost_estimate=pl.CostEstimate(
            flops=2 * ROWS * MODEL * 3 * MODEL, bytes_accessed=8 << 20, transcendentals=0
        ),
    )(attn, tokens, w_out, ln_gain[None], ln_bias[None], w_cross)

    kv = lax.all_to_all(cross_kv, "seq", split_axis=0, concat_axis=0, tiled=True)
    kv = kv.reshape(length, 2 * PAIR)

    blocks = NQ // BLOCK
    keep, send = pl.pallas_call(
        cross_kernel,
        grid_spec=pltpu.PrefetchScalarGridSpec(
            num_scalar_prefetch=1,
            grid=(blocks,),
            in_specs=[
                pl.BlockSpec((NQ, PAIR), lambda b, place: (0, place[0])),
                whole((length, 2 * PAIR)),
            ],
            out_specs=[
                pl.BlockSpec((BLOCK // 2, 2 * PAIR), lambda b, place: (b, 0)),
                pl.BlockSpec((BLOCK // 2, 2 * PAIR), lambda b, place: (b, 0)),
            ],
            scratch_shapes=[
                pltpu.VMEM((PAIR, length), bf16),
                pltpu.VMEM((length, 2 * PAIR), bf16),
                pltpu.VMEM((BLOCK, length), f32),
                pltpu.VMEM((BLOCK, length), f32),
            ],
        ),
        out_shape=[jax.ShapeDtypeStruct((NQ // 2, 2 * PAIR), f32)] * 2,
        compiler_params=params(),
        cost_estimate=pl.CostEstimate(
            flops=8 * NQ * length * 2 * PAIR, bytes_accessed=2 << 20,
            transcendentals=2 * NQ * length,
        ),
    )(place, queries, kv)

    received = permute(send, "span", SPAN, lambda i: i ^ 1)
    merged = pl.pallas_call(
        merge_kernel,
        out_shape=jax.ShapeDtypeStruct((NQ // 2, 2 * PAIR), bf16),
        compiler_params=params(),
    )(keep, received)
    parts = lax.all_to_all(
        merged.reshape(16, OWN, 2 * PAIR),
        "span",
        split_axis=0,
        concat_axis=0,
        tiled=True,
        axis_index_groups=[list(range(0, SPAN, 2)), list(range(1, SPAN, 2))],
    )
    mine = pl.pallas_call(
        finish_kernel,
        out_shape=jax.ShapeDtypeStruct((SEQ, OWN, PAIR), bf16),
        compiler_params=params(),
    )(parts)
    heads = lax.all_to_all(mine, "seq", split_axis=0, concat_axis=0, tiled=True)
    cross_out = jnp.transpose(heads, (1, 0, 2)).reshape(OWN, MODEL)
    return encoded, cross_out


def solution(mesh):
    in_specs = (P(("span", "seq"), None), P("span", None), P(), P(), P(), P(), P())
    out_specs = (P(("span", "seq"), None), P("span", None))
    return jax.shard_map(
        per_device, mesh=mesh, in_specs=in_specs, out_specs=out_specs, check_vma=False
    )
```

```python
import functools
import math

import jax
import jax.numpy as jnp
from jax import lax
from jax.experimental import pallas as pl
from jax.experimental.pallas import tpu as pltpu
from jax.sharding import PartitionSpec as P

H = 16
DH = 64
PAIR = 2 * DH
MODEL = 1024
ROWS = 256
SEQ = 8
SPAN = 32
OWN = 32
NQ = 1024
STAT_LANES = 16
BLOCK = 512
SPREAD = (8, 4, 2, 16)
NEAR, FAR = 5 * ROWS, 3 * ROWS
NEAR_BLOCK, FAR_BLOCK = 640, 384
FAR_PIECES = 4
score_scale = 0.125
LOG2E = math.log2(math.e)
EXP2_SCALE = score_scale * LOG2E

bf16 = jnp.bfloat16
f32 = jnp.float32


def dot(a, b):
    return jnp.dot(a, b, preferred_element_type=f32)


def params(mib=48):
    return pltpu.CompilerParams(vmem_limit_bytes=mib * 1024 * 1024)


def permute(x, axis, size, target):
    return lax.ppermute(x, axis, [(i, target(i)) for i in range(size)])


def lane_low(shape):
    return lax.broadcasted_iota(jnp.int32, shape, len(shape) - 1) < DH


def spread(blocks, bits):
    flips = (bits[0], bits[1], bits[0] | bits[1])
    return jnp.concatenate([blocks] + [permute(blocks, "span", SPAN, lambda i, f=f: i ^ f) for f in flips])


def from_below(x):
    return permute(x, "seq", SEQ, lambda i: (i + 2) % SEQ)


def from_above(x):
    return permute(x, "seq", SEQ, lambda i: (i - 2) % SEQ)


def across(x):
    return permute(x, "seq", SEQ, lambda i: i ^ 1)


def head_scores(q, k_t, head):
    low = lane_low(q.shape)
    zero = jnp.zeros_like(q)
    return dot(jnp.where(low, q, zero) if head == 0 else jnp.where(low, zero, q), k_t)


def weigh(scores, v_ones):
    top = jnp.max(scores, axis=-1, keepdims=True)
    probs = jnp.exp2((scores - top) * EXP2_SCALE).astype(bf16)
    return dot(probs, v_ones), top


def softmax_pair(step, steps, q_block, k_t, v_ones, scores_0, scores_1):
    scores_1[...] = head_scores(q_block(step), k_t[...], 1)
    mixed_0, peak_0 = weigh(scores_0[...], v_ones[...])
    scores_0[...] = head_scores(q_block(jnp.minimum(step + 1, steps - 1)), k_t[...], 0)
    mixed_1, peak_1 = weigh(scores_1[...], v_ones[...])
    low = lane_low((scores_0.shape[0], PAIR))
    total = jnp.where(low, mixed_0[:, PAIR:], mixed_1[:, PAIR:])
    mixed = jnp.where(low, mixed_0[:, :PAIR], mixed_1[:, :PAIR]) / total
    return mixed, jnp.where(low, peak_0, peak_1) * score_scale + jnp.log(total)


def merge_pair(mixed_a, weight_a, mixed_b, weight_b):
    top = jnp.maximum(weight_a, weight_b)
    scale_a, scale_b = jnp.exp(weight_a - top), jnp.exp(weight_b - top)
    total = scale_a + scale_b
    return (mixed_a * scale_a + mixed_b * scale_b) / total, top + jnp.log(total)


def project(pieces, w, q_all, k_t, v_ones, row):
    for piece in pieces:
        count = piece.shape[0]
        block = dot(piece[...], w[...]).astype(bf16)
        q_all[row : row + count, :] = block[:, :PAIR]
        k_t[:, row : row + count] = block[:, PAIR : 2 * PAIR].T
        v_ones[row : row + count, :PAIR] = block[:, 2 * PAIR :]
        row += count
    v_ones[:, PAIR:] = jnp.ones_like(v_ones[:, PAIR:])


def row_block(q_all, size, start=0):
    return lambda i: q_all[pl.ds(pl.multiple_of(start + i * size, 128), size), :]


def near_kernel(
    place, own, peer, up, down, up_far, down_far, mine, twin,
    q_all, k_t, v_ones, w, mixed, weight, scores_0, scores_1,
):
    step = pl.program_id(0)
    q_block = row_block(q_all, NEAR_BLOCK)

    @pl.when(step == 0)
    def _():
        for k in range(1 << len(SPREAD)):
            flip = sum(bit for p, bit in enumerate(SPREAD) if k >> p & 1)
            for core, blocks in enumerate((mine, twin)):
                start = pl.multiple_of((place[1] ^ (flip + core)) * 32, 32)
                w[pl.ds(start, 32), :] = blocks[k * 32 : (k + 1) * 32, :]
        project((own, peer, up, down, up_far, down_far), w, q_all, k_t, v_ones, 0)
        scores_0[...] = head_scores(q_block(0), k_t[...], 0)

    mixed[...], weight[...] = softmax_pair(
        step, NEAR // NEAR_BLOCK, q_block, k_t, v_ones, scores_0, scores_1
    )


def far_kernel(table, *refs):
    pieces, rest = refs[:FAR_PIECES], refs[FAR_PIECES:]
    w, q_near, k_near, v_near, mixed_near, weight_near, out = rest[:7]
    q_far, k_far, v_far, k_t, v_ones, near_0, near_1, far_0, far_1 = rest[7:]
    step = pl.program_id(0)
    near_steps, far_steps = NEAR // NEAR_BLOCK, FAR // FAR_BLOCK
    near_rows, far_rows = row_block(q_near, NEAR_BLOCK), row_block(q_far, FAR_BLOCK)

    def store(mixed, first):
        for c in range(mixed.shape[0] // 128):
            g = first // 128 + c
            start = pl.multiple_of(g % 2 * 128, 128)
            out[table[g // 2], pl.ds(start, 128), :] = mixed[c * 128 : (c + 1) * 128].astype(bf16)

    @pl.when(step == 0)
    def _():
        project(pieces, w, q_far, k_far, v_far, 0)
        k_t[:, :NEAR] = k_near[...]
        k_t[:, NEAR:] = k_far[...]
        v_ones[:NEAR, :] = v_near[...]
        v_ones[NEAR:, :] = v_far[...]
        near_0[...] = head_scores(near_rows(0), k_far[...], 0)

    @pl.when(step < near_steps)
    def _():
        mixed, weight = softmax_pair(step, near_steps, near_rows, k_far, v_far, near_0, near_1)
        rows = pl.ds(pl.multiple_of(step * NEAR_BLOCK, 128), NEAR_BLOCK)
        mixed, _ = merge_pair(mixed, weight, mixed_near[rows, :], weight_near[rows, :])
        store(mixed, step * NEAR_BLOCK)

    @pl.when(step == near_steps)
    def _():
        far_0[...] = head_scores(far_rows(0), k_t[...], 0)

    @pl.when(step >= near_steps)
    def _():
        mixed, _ = softmax_pair(step - near_steps, far_steps, far_rows, k_t, v_ones, far_0, far_1)
        store(mixed, NEAR + (step - near_steps) * FAR_BLOCK)


def encode_kernel(
    attn, tokens, w_out, gain, bias, w_cross_far, encoded, cross_kv, w_cross, arrived
):
    fetch = pltpu.make_async_copy(w_cross_far, w_cross, arrived)
    fetch.start()
    joined = jnp.concatenate([attn[p] for p in range(SEQ)], axis=1)
    residual = tokens[...].astype(f32) + dot(joined, w_out[...])
    center = residual - jnp.mean(residual, -1, keepdims=True)
    spread = jnp.mean(center * center, -1, keepdims=True)
    state = (center * lax.rsqrt(spread + 1e-05) * gain[...] + bias[...]).astype(bf16)
    encoded[...] = state
    fetch.wait()
    for g in range(SEQ // 2):
        for part in range(2):
            start = part * MODEL + 2 * g * PAIR
            both = dot(state, w_cross[:, start : start + 2 * PAIR]).astype(bf16)
            for p in range(2):
                cross_kv[2 * g + p, :, part * PAIR : (part + 1) * PAIR] = both[
                    :, p * PAIR : (p + 1) * PAIR
                ]


def cross_kernel(place, queries, kv, keep, send, k_t, v_ones, scores_0, scores_1):
    step = pl.program_id(0)
    q_block = row_block(queries, BLOCK)

    @pl.when(step == 0)
    def _():
        k_t[...] = kv[:, :PAIR].T
        v_ones[:, :PAIR] = kv[:, PAIR:]
        v_ones[:, PAIR:] = jnp.ones_like(v_ones[:, PAIR:])
        scores_0[...] = head_scores(q_block(0), k_t[...], 0)

    mixed, weight = softmax_pair(
        step, NQ // BLOCK, q_block, k_t, v_ones, scores_0, scores_1
    )
    is_even = place[1] % 2 == 0
    for g in range(BLOCK // (2 * OWN)):
        even = slice(2 * g * OWN, (2 * g + 1) * OWN)
        odd = slice((2 * g + 1) * OWN, (2 * g + 2) * OWN)
        rows = slice(g * OWN, (g + 1) * OWN)
        for lanes, value in ((slice(0, PAIR), mixed), (slice(PAIR, 2 * PAIR), weight)):
            keep[rows, lanes] = jnp.where(is_even, value[even], value[odd])
            send[rows, lanes] = jnp.where(is_even, value[odd], value[even])


def merge_kernel(keep, received, out):
    mixed, weight = merge_pair(keep[:, :PAIR], keep[:, PAIR:], received[:, :PAIR], received[:, PAIR:])
    high = weight.astype(bf16)
    rest = weight - high.astype(f32)
    middle = rest.astype(bf16)
    low = (rest - middle.astype(f32)).astype(bf16)
    part = lax.broadcasted_iota(jnp.int32, weight.shape, 1) % DH // STAT_LANES
    out[:, :PAIR] = mixed.astype(bf16)
    out[:, PAIR:] = jnp.where(part == 0, high, jnp.where(part == 1, middle, low))


def finish_kernel(parts, out):
    stat = parts[:, :, PAIR:].astype(f32)
    low = lane_low(stat.shape)
    columns = []
    for h in range(2):
        high, middle, rest = (
            stat[:, :, h * DH + p * STAT_LANES : h * DH + p * STAT_LANES + 1] for p in range(3)
        )
        columns.append(high + (middle + rest))
    weight = jnp.where(low, columns[0], columns[1])
    scale = jnp.exp(weight - jnp.max(weight, axis=0, keepdims=True))
    mixed = jnp.sum(parts[:, :, :PAIR].astype(f32) * scale, axis=0) / jnp.sum(scale, axis=0)
    out[...] = jnp.broadcast_to(mixed.astype(bf16)[None], out.shape)


def per_device(tokens, w_qkv, w_out, w_cross, ln_gain, ln_bias, queries):
    seq_index = lax.axis_index("seq")
    span_index = lax.axis_index("span")
    y, x_lo = seq_index // 2, seq_index % 2

    half = ROWS // 2
    peer, up, down = across(tokens), from_below(tokens), from_above(tokens)
    mine = jnp.concatenate(
        [
            lax.dynamic_slice_in_dim(w_qkv, part * MODEL + seq_index * PAIR, PAIR, 1)
            for part in range(3)
        ],
        axis=1,
    )
    for bit in SPREAD[:2]:
        mine = jnp.concatenate([mine, permute(mine, "span", SPAN, lambda i, f=bit: i ^ f)])
    peer, up, down, mine = lax.optimization_barrier((peer, up, down, mine))
    near = (up, down, from_below(up[:half]), from_above(down[half:]))
    mine = spread(mine, SPREAD[2:])
    peer, mine = lax.optimization_barrier((peer, mine))
    far = (from_below(peer), from_above(peer), across(near[2]), across(near[3]))
    twin = permute(mine, "span", SPAN, lambda i: i ^ 1)

    def whole(shape):
        return pl.BlockSpec(shape, lambda *_: (0,) * len(shape))

    place = jnp.stack([seq_index, span_index]).astype(jnp.int32)
    length = SEQ * ROWS
    shapes = [
        jax.ShapeDtypeStruct((NEAR, PAIR), bf16),
        jax.ShapeDtypeStruct((PAIR, NEAR), bf16),
        jax.ShapeDtypeStruct((NEAR, 2 * PAIR), bf16),
        jax.ShapeDtypeStruct((MODEL, 3 * PAIR), bf16),
        jax.ShapeDtypeStruct((NEAR, PAIR), f32),
        jax.ShapeDtypeStruct((NEAR, PAIR), f32),
    ]
    pieces = (tokens, peer, *near, mine, twin)
    q_near, k_near, v_near, weight, mixed_near, weight_near = pl.pallas_call(
        near_kernel,
        grid=(NEAR // NEAR_BLOCK,),
        in_specs=[pl.BlockSpec(memory_space=pltpu.SMEM)] + [whole(p.shape) for p in pieces],
        out_specs=[whole(p.shape) for p in shapes[:4]]
        + [pl.BlockSpec((NEAR_BLOCK, PAIR), lambda b: (b, 0))] * 2,
        out_shape=shapes,
        scratch_shapes=[pltpu.VMEM((NEAR_BLOCK, NEAR), f32)] * 2,
        compiler_params=params(28),
        cost_estimate=pl.CostEstimate(
            flops=2 * NEAR * MODEL * 3 * PAIR, bytes_accessed=4 << 20, transcendentals=0
        ),
    )(place, *pieces)

    order = jnp.stack(
        [((y + dy) % 4) * 2 + (x_lo ^ flip) for dy, flip in
         ((0, 0), (0, 1), (3, 0), (1, 0), (2, 0), (3, 1), (1, 1), (2, 1))]
    ).astype(jnp.int32)
    operands = (*far, weight, q_near, k_near, v_near, mixed_near, weight_near)
    attn = pl.pallas_call(
        far_kernel,
        grid_spec=pltpu.PrefetchScalarGridSpec(
            num_scalar_prefetch=1,
            grid=(NEAR // NEAR_BLOCK + FAR // FAR_BLOCK,),
            in_specs=[whole(p.shape) for p in operands],
            out_specs=whole((SEQ, ROWS, PAIR)),
            scratch_shapes=[
                pltpu.VMEM((FAR, PAIR), bf16),
                pltpu.VMEM((PAIR, FAR), bf16),
                pltpu.VMEM((FAR, 2 * PAIR), bf16),
                pltpu.VMEM((PAIR, length), bf16),
                pltpu.VMEM((length, 2 * PAIR), bf16),
                pltpu.VMEM((NEAR_BLOCK, FAR), f32),
                pltpu.VMEM((NEAR_BLOCK, FAR), f32),
                pltpu.VMEM((FAR_BLOCK, length), f32),
                pltpu.VMEM((FAR_BLOCK, length), f32),
            ],
        ),
        out_shape=jax.ShapeDtypeStruct((SEQ, ROWS, PAIR), bf16),
        compiler_params=params(32),
        cost_estimate=pl.CostEstimate(
            flops=6 * length * length * 2 * PAIR, bytes_accessed=4 << 20,
            transcendentals=2 * length * length,
        ),
    )(order, *operands)
    attn = lax.all_to_all(attn, "seq", split_axis=0, concat_axis=0, tiled=True)

    encoded, cross_kv = pl.pallas_call(
        encode_kernel,
        in_specs=[pl.BlockSpec(memory_space=pltpu.VMEM)] * 5 + [pl.BlockSpec(memory_space=pl.ANY)],
        scratch_shapes=[pltpu.VMEM((MODEL, 2 * MODEL), bf16), pltpu.SemaphoreType.DMA],
        out_shape=[
            jax.ShapeDtypeStruct((ROWS, MODEL), bf16),
            jax.ShapeDtypeStruct((SEQ, ROWS, 2 * PAIR), bf16),
        ],
        compiler_params=params(),
        cost_estimate=pl.CostEstimate(
            flops=2 * ROWS * MODEL * 3 * MODEL, bytes_accessed=8 << 20, transcendentals=0
        ),
    )(attn, tokens, w_out, ln_gain[None], ln_bias[None], w_cross)

    kv = lax.all_to_all(cross_kv, "seq", split_axis=0, concat_axis=0, tiled=True)
    kv = kv.reshape(length, 2 * PAIR)

    blocks = NQ // BLOCK
    keep, send = pl.pallas_call(
        cross_kernel,
        grid_spec=pltpu.PrefetchScalarGridSpec(
            num_scalar_prefetch=1,
            grid=(blocks,),
            in_specs=[
                pl.BlockSpec((NQ, PAIR), lambda b, place: (0, place[0])),
                whole((length, 2 * PAIR)),
            ],
            out_specs=[
                pl.BlockSpec((BLOCK // 2, 2 * PAIR), lambda b, place: (b, 0)),
                pl.BlockSpec((BLOCK // 2, 2 * PAIR), lambda b, place: (b, 0)),
            ],
            scratch_shapes=[
                pltpu.VMEM((PAIR, length), bf16),
                pltpu.VMEM((length, 2 * PAIR), bf16),
                pltpu.VMEM((BLOCK, length), f32),
                pltpu.VMEM((BLOCK, length), f32),
            ],
        ),
        out_shape=[jax.ShapeDtypeStruct((NQ // 2, 2 * PAIR), f32)] * 2,
        compiler_params=params(),
        cost_estimate=pl.CostEstimate(
            flops=8 * NQ * length * 2 * PAIR, bytes_accessed=2 << 20,
            transcendentals=2 * NQ * length,
        ),
    )(place, queries, kv)

    received = permute(send, "span", SPAN, lambda i: i ^ 1)
    merged = pl.pallas_call(
        merge_kernel,
        out_shape=jax.ShapeDtypeStruct((NQ // 2, 2 * PAIR), bf16),
        compiler_params=params(),
    )(keep, received)
    parts = lax.all_to_all(
        merged.reshape(16, OWN, 2 * PAIR),
        "span",
        split_axis=0,
        concat_axis=0,
        tiled=True,
        axis_index_groups=[list(range(0, SPAN, 2)), list(range(1, SPAN, 2))],
    )
    mine = pl.pallas_call(
        finish_kernel,
        out_shape=jax.ShapeDtypeStruct((SEQ, OWN, PAIR), bf16),
        compiler_params=params(),
    )(parts)
    heads = lax.all_to_all(mine, "seq", split_axis=0, concat_axis=0, tiled=True)
    cross_out = jnp.transpose(heads, (1, 0, 2)).reshape(OWN, MODEL)
    return encoded, cross_out


def solution(mesh):
    in_specs = (P(("span", "seq"), None), P("span", None), P(), P(), P(), P(), P())
    out_specs = (P(("span", "seq"), None), P("span", None))
    return jax.shard_map(
        per_device, mesh=mesh, in_specs=in_specs, out_specs=out_specs, check_vma=False
    )
```
